32 devices in a mesh: groups: 2 (over y), fsdp: 4 (over z), replica: 4 (over x, core).
Axes of the slice: x: 2, y: 2, z: 4, core: 2. Of those that a mesh axis runs over, the one named last changes fastest.
Arguments:
- hidden: bfloat16 [4, 3072, 2560], P('replica', ('groups', 'fsdp')), parts along dimension 1, may hold values from -6 to 6
- targets: int32 [4, 3072], P('replica', ('groups', 'fsdp')), parts along dimension 1, may hold values from 0 to 440
- params: float32 [4, 5120, 441], P('replica', ('groups', 'fsdp')), parts along dimension 1, may hold values from -0.875 to 0.875
- moment: float32 [4, 5120, 441], P('replica', ('groups', 'fsdp')), parts along dimension 1, may hold values from -24 to 24
- second: float32 [4, 5120, 441], P('replica', ('groups', 'fsdp')), parts along dimension 1, may hold values from 1 to 100
- train_step: int32 [1], replicated, may hold values from 1 to 99999
Outputs:
- averaged: float32 [4, 5120, 441], P('replica', ('groups', 'fsdp')), parts along dimension 1
- moment_new: float32 [4, 5120, 441], P('replica', ('groups', 'fsdp')), parts along dimension 1
- second_new: float32 [4, 5120, 441], P('replica', ('groups', 'fsdp')), parts along dimension 1
- grad_hidden: bfloat16 [4, 3072, 2560], P('replica', ('groups', 'fsdp')), parts along dimension 1
The draws below stay inside these ranges and needn't reach their ends.
There are 2 independent parts, one for each index of `groups`. The reference program is written for one: setup_inputs(seed, part) draws one part's arguments, and reference() takes and returns one part's arrays. A program takes and returns all parts, laid end to end along the dimension named above; an argument that names none is the same for every part. Nothing has to cross between parts.
All inputs are finite; a program needn't handle non-finite values.
Results may differ from the reference program's by a relative error of at most 0.0049.
The reference program's roundings to bfloat16 on the way (of `normed_bf`, `weight_bf` and `logit_grad`) count: a program that leaves them out, or rounds other values in their place, can miss the bound.
Values may be sent and summed in bfloat16 or wider, within the bound.
No kernel may reach another device: no remote copies, remote signals or barrier semaphores. Data moves between devices by JAX's collectives and lax.ppermute only.
A program may use at most 64 MiB of HBM per device.

```python
import math
import jax
import jax.numpy as jnp
import numpy as np
from jax import lax

D = 2560
V = 441
TOK_DEV = 384
REPLICAS = 4
TOKENS = 1536
N_FSDP = 4


def touch_ends(result, own_key, least, top_value):
    place = [jax.random.randint(jax.random.fold_in(own_key, axis), (), 0, length) for axis, length in enumerate(result.shape)]
    longest = result.shape.index(max(result.shape))
    next_to = place[:longest] + [(place[longest] + 1) % result.shape[longest]] + place[longest + 1:]
    return result.at[tuple(place)].set(least).at[tuple(next_to)].set(top_value)


def with_spikes(array, rng, source, target, parts, factor):
    owner, partner = [(jnp.arange(array.shape[dim]) // (array.shape[dim] // parts)).reshape([-1 if axis == dim else 1 for axis in range(array.ndim)]) for dim in (source, target)]
    chosen = jax.random.permutation(rng, parts)[partner]
    strong = (owner == chosen) | (owner == (partner + parts // 2) % parts)
    return jnp.where(strong, factor * array, array)


def level_of(key, extent, pieces, least, high):
    level, own = 1.0, jax.random.fold_in(key, 6)
    for axis_at, blocks in pieces:
        draws = jnp.exp(jax.random.uniform(jax.random.fold_in(own, axis_at), (blocks,), jnp.float32, least / len(pieces), high / len(pieces)))
        level = level * jnp.repeat(draws, extent[axis_at] // blocks).reshape([-1 if axis == axis_at else 1 for axis in range(len(extent))])
    return level


def rank_table(count, lean):
    loads = [(1 << 20) // math.isqrt(standing ** lean) + 1 for standing in range(1, count + 1)]
    deviation = 1 + sum(loads) // (1 << 30)
    return np.cumsum(np.array([max(1, weight // deviation) for weight in loads]))


def ranked(key, extent, amount, skew):
    listing = rank_table(amount, skew)
    lot = jax.random.randint(jax.random.fold_in(key, 1), extent, 0, int(listing[amount - 1]))
    grade = jnp.searchsorted(jnp.asarray(listing, jnp.int32), lot, side="right")
    return jax.random.permutation(jax.random.fold_in(key, 2), amount)[grade].astype(jnp.int32)


def bell_draw(rng, extent, deviation, limit, pieces=(), held_as=jnp.bfloat16):
    level = level_of(rng, extent, pieces, -0.22, 0.18) if pieces else 1.0
    drawn = jax.random.normal(rng, extent, jnp.float32) * deviation * level
    return jnp.minimum(jnp.maximum(drawn, -limit), limit).astype(held_as)


def bell_draw_with(stream_key, shape, deviation, bound, split, heavy, held_as=jnp.bfloat16):
    result = deviation * jax.random.normal(stream_key, shape, jnp.float32)
    if split:
        result = result * level_of(stream_key, shape, split, -0.22, 0.18)
    return jnp.clip(with_spikes(result, jax.random.fold_in(stream_key, 3), *heavy), -bound, bound).astype(held_as)


def setup_inputs(seed: int = 0, part: int = 0) -> dict:
    key_list = jax.random.split(jax.random.key(seed), 7)
    own_keys = jax.random.split(jax.random.fold_in(key_list[6], part), 7)
    hidden = bell_draw_with(own_keys[0], (REPLICAS, TOKENS, D), 1.0, 6.0, ((0, 4), (1, 4)), (1, 2, 4, 2.0))
    targets = touch_ends(ranked(own_keys[1], (REPLICAS, TOKENS), V, 2), jax.random.fold_in(own_keys[1], 3), 0, V - 1).astype(jnp.int32)
    params = bell_draw(own_keys[2], (REPLICAS, D, V), 0.06, 0.875, ((0, 4), (1, 4)), jnp.float32)
    moment = bell_draw(own_keys[3], (REPLICAS, D, V), 4.0, 24.0, ((0, 4), (1, 4)), jnp.float32)
    second = jnp.clip(jnp.exp(math.log(100.0) - 4.6051702 * jax.random.uniform(own_keys[4], (REPLICAS, D, V), jnp.float32) ** level_of(own_keys[4], (REPLICAS, D, V), ((0, 4), (1, 4)), -0.2, 0.2)), 1.0, 100.0)
    train_step = jax.random.randint(key_list[5], (1,), 1, 100000).astype(jnp.int32)
    return dict(hidden=hidden, targets=targets, params=params, moment=moment, second=second, train_step=train_step)


norm_eps = 1e-05
logit_cap = 30.0
learn_rate = 0.001
weight_decay = 0.1
beta_one = 0.9
beta_two = 0.999
adam_eps = 1e-08

def normalize(token_block):
    values = token_block.astype(jnp.float32)
    center = values - lax.optimization_barrier(jnp.mean(values, axis=-1, keepdims=True))
    inv_scale = lax.rsqrt(lax.optimization_barrier(jnp.mean(center * center, axis=-1, keepdims=True)) + norm_eps)
    return (center * inv_scale, inv_scale)

def head_block(token_block, labels, weight_bf):
    normalized, inv_scale = normalize(token_block)
    normed_bf = normalized.astype(jnp.bfloat16)
    raw_logits = jnp.dot(normed_bf, weight_bf, preferred_element_type=jnp.float32)
    capped = jnp.tanh(raw_logits / logit_cap)
    exp_logits = jnp.exp(logit_cap * capped)
    softmax_p = exp_logits / lax.optimization_barrier(jnp.sum(exp_logits, axis=-1, keepdims=True))
    onehot = (labels[:, None] == jnp.arange(weight_bf.shape[1], dtype=jnp.int32)[None, :]).astype(jnp.float32)
    logit_grad = ((softmax_p - onehot) * (1.0 - capped * capped)).astype(jnp.bfloat16)
    part_grad = lax.dot_general(normed_bf, logit_grad, (((0,), (0,)), ((), ())), preferred_element_type=jnp.float32)
    normed_grad = lax.dot_general(logit_grad, weight_bf, (((1,), (1,)), ((), ())), preferred_element_type=jnp.float32)
    first_mean = lax.optimization_barrier(jnp.mean(normed_grad, axis=-1, keepdims=True))
    second_mean = lax.optimization_barrier(jnp.mean(normed_grad * normalized, axis=-1, keepdims=True))
    grad_hidden = inv_scale * (normed_grad - first_mean - normalized * second_mean)
    return (part_grad.astype(jnp.bfloat16), grad_hidden.astype(jnp.bfloat16))

def replica_pass(replica_item):
    hidden, targets, weight = replica_item
    weight_bf = weight.astype(jnp.bfloat16)
    blocks = hidden.reshape(N_FSDP, TOK_DEV, D)
    labels = targets.reshape(N_FSDP, TOK_DEV)

    def add_block(grad_total, block_pair):
        part_grad, grad_hidden = head_block(block_pair[0], block_pair[1], weight_bf)
        part_grad = lax.optimization_barrier(part_grad)
        return (grad_total + part_grad.astype(jnp.float32), grad_hidden)
    grads, backs = lax.scan(add_block, jnp.zeros((D, V), jnp.float32), (blocks, labels))
    return (grads, backs.reshape(TOKENS, D))

def reference(hidden, targets, params, moment, second, train_step):
    replica_grads, grad_hidden = lax.map(replica_pass, (hidden, targets, params))
    tcount = train_step[0].astype(jnp.float32)
    fix_one = 1.0 - jnp.exp(tcount * math.log(beta_one))
    fix_two = 1.0 - jnp.exp(tcount * math.log(beta_two))
    moment_new = beta_one * moment + (1.0 - beta_one) * replica_grads
    second_new = beta_two * second + (1.0 - beta_two) * replica_grads * replica_grads
    adam_step = moment_new / fix_one / (jnp.sqrt(second_new / fix_two) + adam_eps)
    updated = params - learn_rate * (adam_step + weight_decay * params)
    levels = int(REPLICAS).bit_length() - 1
    distance = jnp.left_shift(jnp.int32(1), (train_step[0] % levels).astype(jnp.int32))
    partner = jnp.bitwise_xor(jnp.arange(REPLICAS, dtype=jnp.int32), distance)
    averaged = 0.5 * (updated + jnp.take(updated, partner, axis=0))
    return (averaged, moment_new, second_new, grad_hidden)
```

```python
import math

import jax
import jax.numpy as jnp
from jax import lax
from jax.experimental import pallas as pl
from jax.experimental.pallas import tpu as pltpu
from jax.sharding import PartitionSpec as P

norm_eps = 1e-05
logit_cap = 30.0
learn_rate = 0.001
weight_decay = 0.1
beta_one = 0.9
beta_two = 0.999
adam_eps = 1e-08


def shortened(x):
    return jax.tree.map(lambda a: a.astype(jnp.bfloat16) if a.dtype == jnp.float32 else a, x)


def from_partner(block, axis, stride):
    count = lax.axis_size(axis)
    route = []
    for low in range(count):
        high = low | 1 << stride
        if high != low and high < count:
            route += [(low, high), (high, low)]
    return lax.ppermute(block, axis, route)


def normalize(token_block):
    values = token_block.astype(jnp.float32)
    center = values - jnp.mean(values, axis=-1, keepdims=True)
    inv_scale = lax.rsqrt(jnp.mean(center * center, axis=-1, keepdims=True) + norm_eps)
    return (center * inv_scale, inv_scale)


def pair_with(bit_index):

    def swap_values(values):
        return jax.tree.map(
            lambda part, own: part.astype(own.dtype),
            from_partner(shortened(values), "replica", bit_index),
            values,
        )

    return swap_values


def local_any(hidden, targets, params, moment, second, train_step):
    normalized, inv_scale = normalize(hidden[0])
    normed_bf = normalized.astype(jnp.bfloat16)
    labels = targets[0]
    shard_bf = params[0].astype(jnp.bfloat16)
    vocab_width = shard_bf.shape[1]
    weight_bf = lax.all_gather(shard_bf, "fsdp", axis=0, tiled=True)
    raw_logits = jnp.dot(normed_bf, weight_bf, preferred_element_type=jnp.float32)
    capped = jnp.tanh(raw_logits / logit_cap)
    exp_logits = jnp.exp(logit_cap * capped)
    softmax_p = exp_logits / jnp.sum(exp_logits, axis=-1, keepdims=True)
    onehot = (labels[:, None] == jnp.arange(vocab_width, dtype=jnp.int32)[None, :]).astype(
        jnp.float32
    )
    logit_grad = ((softmax_p - onehot) * (1.0 - capped * capped)).astype(jnp.bfloat16)
    full_grad = lax.dot_general(
        normed_bf, logit_grad, (((0,), (0,)), ((), ())), preferred_element_type=jnp.float32
    )
    grad_shard = lax.psum_scatter(
        full_grad.astype(jnp.bfloat16), "fsdp", scatter_dimension=0, tiled=True
    ).astype(jnp.float32)
    normed_grad = lax.dot_general(
        logit_grad, weight_bf, (((1,), (1,)), ((), ())), preferred_element_type=jnp.float32
    )
    first_mean = jnp.mean(normed_grad, axis=-1, keepdims=True)
    second_mean = jnp.mean(normed_grad * normalized, axis=-1, keepdims=True)
    grad_hidden = (inv_scale * (normed_grad - first_mean - normalized * second_mean)).astype(
        jnp.bfloat16
    )
    tcount = train_step[0].astype(jnp.float32)
    fix_one = 1.0 - jnp.exp(tcount * math.log(beta_one))
    fix_two = 1.0 - jnp.exp(tcount * math.log(beta_two))
    replica_grads = grad_shard[None]
    moment_new = beta_one * moment + (1.0 - beta_one) * replica_grads
    second_new = beta_two * second + (1.0 - beta_two) * replica_grads * replica_grads
    adam_step = moment_new / fix_one / (jnp.sqrt(second_new / fix_two) + adam_eps)
    updated = params - learn_rate * (adam_step + weight_decay * params)
    levels = lax.axis_size("replica").bit_length() - 1
    partner_values = lax.switch(
        train_step[0] % levels, [pair_with(bit_index) for bit_index in range(levels)], updated
    )
    averaged = 0.5 * (updated + partner_values)
    return (averaged, moment_new, second_new, grad_hidden[None])


near_route = [(0, 1), (1, 0), (2, 3), (3, 2)]
far_route = [(0, 2), (2, 0), (1, 3), (3, 1)]
mid_route = [(1, 2), (2, 1)]
outward_route = [(1, 0), (2, 3)]
inward_route = [(0, 1), (3, 2)]

f32 = jnp.float32
bf16 = jnp.bfloat16
vmem = pl.BlockSpec(memory_space=pltpu.VMEM)
smem = pl.BlockSpec(memory_space=pltpu.SMEM)
anywhere = pl.BlockSpec(memory_space=pl.ANY)


def shaped(shape, dtype):
    return jax.ShapeDtypeStruct(shape, dtype)


def run(kernel, ins, outs, args, scratch=(), limit=24, flops=0, moved=0):
    single = not isinstance(outs, (list, tuple))
    out_specs = vmem if single else [vmem] * len(outs)
    return pl.pallas_call(
        kernel,
        in_specs=ins,
        out_specs=out_specs,
        out_shape=outs,
        scratch_shapes=list(scratch),
        compiler_params=pltpu.CompilerParams(vmem_limit_bytes=limit << 20),
        cost_estimate=pl.CostEstimate(flops=flops, bytes_accessed=moved, transcendentals=0),
    )(*args)


def columns(block, width):
    return pl.ds(pl.multiple_of(block * width, 128), width)


def nt_dot(a, b):
    return lax.dot_general(a, b, (((1,), (1,)), ((), ())), preferred_element_type=f32)


def tn_dot(a, b):
    return lax.dot_general(a, b, (((0,), (0,)), ((), ())), preferred_element_type=f32)


def round_weight_kernel(params_ref, out_ref, held, sem):
    vocab = held.shape[0]
    copy = pltpu.make_async_copy(params_ref.at[:, 0, :], held, sem)
    copy.start()
    copy.wait()
    out_ref[0:vocab, :] = held[...].astype(bf16)
    out_ref[vocab:, :] = jnp.zeros((out_ref.shape[0] - vocab, out_ref.shape[1]), bf16)


def norm_kernel(place_ref, hidden_ref, normed_ref, mean_ref, inv_ref):
    rows, width = hidden_ref.shape
    depth = normed_ref.shape[2]
    step = 128
    for top in range(0, rows, step):
        part = pl.ds(top, step)
        values = hidden_ref[part, :].astype(f32)
        mean = jnp.mean(values, axis=-1, keepdims=True)
        center = values - mean
        inv = lax.rsqrt(jnp.mean(center * center, axis=-1, keepdims=True) + norm_eps)
        mean_ref[part, :] = mean
        inv_ref[part, :] = inv
        for slot in range(normed_ref.shape[0]):
            block = place_ref[0] ^ slot
            own = hidden_ref[part, columns(block, depth)].astype(f32)
            normed_ref[slot, part, :] = ((own - mean) * inv).astype(bf16)


def partial_kernel(own_ref, near_ref, far_ref, normed_ref, acc_ref):
    acc = nt_dot(own_ref[...], normed_ref[0])
    acc = acc + nt_dot(near_ref[...], normed_ref[1])
    acc_ref[...] = acc + nt_dot(far_ref[...], normed_ref[2])


def cross_block(place_ref, mid_ref, outer_ref):
    middle = (place_ref[0] == 1) | (place_ref[0] == 2)
    return jnp.where(middle, mid_ref[...], outer_ref[...])


def head_kernel(vocab, place_ref, acc_ref, mid_ref, outer_ref, normed_ref, labels_ref, lg_ref, cross_ref):
    raw = acc_ref[...] + nt_dot(cross_block(place_ref, mid_ref, outer_ref), normed_ref[3])
    capped = jnp.tanh(raw / logit_cap)
    ids = lax.broadcasted_iota(jnp.int32, raw.shape, 0)
    exp_logits = jnp.where(ids < vocab, jnp.exp(logit_cap * capped), 0.0)
    softmax_p = exp_logits / jnp.sum(exp_logits, axis=0, keepdims=True)
    onehot = (ids == labels_ref[...]).astype(f32)
    logit_grad = ((softmax_p - onehot) * (1.0 - capped * capped)).astype(bf16)
    lg_ref[...] = logit_grad
    cross_ref[...] = jnp.dot(logit_grad, normed_ref[3], preferred_element_type=f32).astype(bf16)


def grads_kernel(lg_ref, normed_ref, own_ref, near_ref, far_ref):
    for slot, out in enumerate((own_ref, near_ref, far_ref)):
        out[...] = jnp.dot(lg_ref[...], normed_ref[slot], preferred_element_type=f32).astype(bf16)


def add_kernel(a_ref, b_ref, out_ref):
    out_ref[...] = (a_ref[...].astype(f32) + b_ref[...].astype(f32)).astype(bf16)


def hidden_grad_kernel(
    place_ref, lg_ref, own_ref, near_ref, far_ref, mid_ref, outer_ref, hidden_ref, mean_ref, inv_ref, out_ref, held
):
    rows, width = hidden_ref.shape
    slots, _, depth = held.shape
    mean, inv = mean_ref[...], inv_ref[...]
    first = jnp.zeros((rows, 1), f32)
    second = jnp.zeros((rows, 1), f32)
    for slot in range(slots):
        if slot == 3:
            block = cross_block(place_ref, mid_ref, outer_ref)
        else:
            block = (own_ref, near_ref, far_ref)[slot][...]
        back = tn_dot(lg_ref[...], block)
        held[slot] = back
        normalized = (hidden_ref[:, columns(place_ref[0] ^ slot, depth)].astype(f32) - mean) * inv
        first = first + jnp.sum(back, axis=-1, keepdims=True)
        second = second + jnp.sum(back * normalized, axis=-1, keepdims=True)
    first, second = first / width, second / width
    for slot in range(slots):
        part = columns(place_ref[0] ^ slot, depth)
        normalized = (hidden_ref[:, part].astype(f32) - mean) * inv
        out_ref[:, part] = (inv * (held[slot] - first - normalized * second)).astype(bf16)


def summed_grads(vocab, refs):
    return sum(ref[0:vocab, :].astype(f32) for ref in refs)


def step_kernel(fix_ref, own_ref, near_ref, far_ref, mid_ref, params_ref, moment_ref, second_ref,
                updated_ref, sent_ref, sems, params_in, moment_in, second_in):
    vocab = updated_ref.shape[0]
    copies = []
    for slot, (src, dst) in enumerate(
        ((moment_ref, moment_in), (second_ref, second_in), (params_ref, params_in))
    ):
        copies.append(pltpu.make_async_copy(src.at[:, 0, :], dst, sems.at[slot]))
        copies[-1].start()
    for copy in copies:
        copy.wait()
    grads = summed_grads(vocab, (own_ref, near_ref, far_ref, mid_ref))
    moment_new = beta_one * moment_in[...] + (1.0 - beta_one) * grads
    second_new = beta_two * second_in[...] + (1.0 - beta_two) * grads * grads
    adam_step = moment_new / fix_ref[0] / (jnp.sqrt(second_new / fix_ref[1]) + adam_eps)
    params = params_in[...]
    updated = params - learn_rate * (adam_step + weight_decay * params)
    updated_ref[...] = updated
    sent_ref[0:vocab, :] = updated.astype(bf16)
    sent_ref[vocab:, :] = jnp.zeros((sent_ref.shape[0] - vocab, sent_ref.shape[1]), bf16)


def moments_kernel(own_ref, near_ref, far_ref, mid_ref, moment_ref, second_ref, moment_out, second_out,
                   sems, moment_in, second_in):
    vocab = moment_in.shape[0]
    into = [
        pltpu.make_async_copy(moment_ref.at[:, 0, :], moment_in, sems.at[0]),
        pltpu.make_async_copy(second_ref.at[:, 0, :], second_in, sems.at[1]),
    ]
    for copy in into:
        copy.start()
    for copy in into:
        copy.wait()
    grads = summed_grads(vocab, (own_ref, near_ref, far_ref, mid_ref))
    moment_in[...] = beta_one * moment_in[...] + (1.0 - beta_one) * grads
    back = [pltpu.make_async_copy(moment_in, moment_out.at[:, 0, :], sems.at[0])]
    back[0].start()
    second_in[...] = beta_two * second_in[...] + (1.0 - beta_two) * grads * grads
    back.append(pltpu.make_async_copy(second_in, second_out.at[:, 0, :], sems.at[1]))
    back[1].start()
    for copy in back:
        copy.wait()


def average_kernel(updated_ref, partner_ref, out_ref, sem, held):
    vocab = held.shape[0]
    held[...] = 0.5 * (updated_ref[...] + partner_ref[0:vocab, :].astype(f32))
    copy = pltpu.make_async_copy(held, out_ref.at[:, 0, :], sem)
    copy.start()
    copy.wait()


def by_vocab(shard):
    return jnp.transpose(shard, (2, 0, 1))


def local_line(hidden, targets, params, moment, second, train_step):
    tokens, width = hidden.shape[1:]
    depth, vocab = params.shape[1:]
    padded = -(-vocab // 16) * 16
    place = lax.axis_index("fsdp")[None]
    params_t, moment_t, second_t = by_vocab(params), by_vocab(moment), by_vocab(second)
    shard = shaped((padded, depth), bf16)
    state = pltpu.VMEM((vocab, depth), f32)
    state_out = shaped((vocab, 1, depth), f32)
    dma = pltpu.SemaphoreType.DMA
    dot_flops = 2 * padded * tokens * depth

    own = run(round_weight_kernel, [anywhere], shard, (params_t,), [state, dma])
    far = lax.ppermute(own, "fsdp", far_route)
    near = lax.ppermute(own, "fsdp", near_route)
    normed, mean, inv = run(
        norm_kernel,
        [smem, vmem],
        [shaped((4, tokens, depth), bf16), shaped((tokens, 1), f32), shaped((tokens, 1), f32)],
        (place, hidden[0]),
        flops=10 * tokens * width,
        moved=4 * tokens * width,
    )
    own_late, far = lax.optimization_barrier((own, far))
    mid = lax.ppermute(own_late, "fsdp", mid_route)
    outer = lax.ppermute(far, "fsdp", outward_route)
    acc = run(
        partial_kernel, [vmem] * 4, shaped((padded, tokens), f32), (own, near, far, normed), flops=3 * dot_flops
    )
    lg, cross_part = run(
        lambda *refs: head_kernel(vocab, *refs),
        [smem] + [vmem] * 5,
        [shaped((padded, tokens), bf16), shard],
        (place, acc, mid, outer, normed, targets),
        flops=2 * dot_flops,
    )
    got_mid = lax.ppermute(cross_part, "fsdp", mid_route)
    got_in = lax.ppermute(cross_part, "fsdp", inward_route)
    own_part, near_part, far_part = run(
        grads_kernel, [vmem] * 2, [shard] * 3, (lg, normed), flops=3 * dot_flops
    )
    far_sum = run(add_kernel, [vmem] * 2, shard, (far_part, got_in))
    got_far = lax.ppermute(far_sum, "fsdp", far_route)
    near_part, _ = lax.optimization_barrier((near_part, got_in))
    got_near = lax.ppermute(near_part, "fsdp", near_route)
    grad_hidden = run(
        hidden_grad_kernel,
        [smem] + [vmem] * 9,
        shaped((tokens, width), bf16),
        (place, lg, own, near, far, mid, outer, hidden[0], mean, inv),
        [pltpu.VMEM((4, tokens, depth), f32)],
        flops=4 * dot_flops,
    )
    tcount = train_step[0].astype(f32)
    fix = jnp.stack([1.0 - jnp.exp(tcount * math.log(beta_one)), 1.0 - jnp.exp(tcount * math.log(beta_two))])
    parts = (own_part, got_near, got_far, got_mid)
    updated, sent = run(
        step_kernel,
        [smem] + [vmem] * 4 + [anywhere] * 3,
        [shaped((vocab, depth), f32), shard],
        (fix, *parts, params_t, moment_t, second_t),
        [dma((3,)), state, state, state],
    )

    def pair_with_bit(bit_index):
        def finish(updated, sent, parts, moment_t, second_t):
            partner = from_partner(sent, "replica", bit_index)
            moment_new, second_new = run_out(
                moments_kernel,
                [vmem] * 4 + [anywhere] * 2,
                [state_out] * 2,
                (*parts, moment_t, second_t),
                [dma((2,)), state, state],
            )
            averaged = run_out(
                average_kernel, [vmem] * 2, [state_out], (updated, partner), [dma, state]
            )[0]
            return averaged, moment_new, second_new

        return finish

    levels = lax.axis_size("replica").bit_length() - 1
    outs = lax.switch(
        train_step[0] % levels,
        [pair_with_bit(bit_index) for bit_index in range(levels)],
        updated, sent, parts, moment_t, second_t,
    )
    averaged, moment_new, second_new = (jnp.transpose(out, (1, 2, 0)) for out in outs)
    return (averaged, moment_new, second_new, grad_hidden[None])


def run_out(kernel, ins, outs, args, scratch):
    return pl.pallas_call(
        kernel,
        in_specs=ins,
        out_specs=[anywhere] * len(outs),
        out_shape=outs,
        scratch_shapes=list(scratch),
        compiler_params=pltpu.CompilerParams(vmem_limit_bytes=24 << 20),
        cost_estimate=pl.CostEstimate(flops=0, bytes_accessed=6 << 20, transcendentals=0),
    )(*args)


def local(hidden, targets, params, moment, second, train_step):
    four = lax.axis_size("fsdp") == 4 and params.shape[1] % 128 == 0 and hidden.shape[1] % 128 == 0
    chosen = local_line if four else local_any
    return chosen(hidden, targets, params, moment, second, train_step)


def solution(mesh):
    placed = (
        P("replica", ("groups", "fsdp"), None),
        P("replica", ("groups", "fsdp")),
        P("replica", ("groups", "fsdp"), None),
        P("replica", ("groups", "fsdp"), None),
        P("replica", ("groups", "fsdp"), None),
        P(),
    )
    return jax.shard_map(
        local,
        mesh=mesh,
        in_specs=placed,
        out_specs=(
            P("replica", ("groups", "fsdp"), None),
            P("replica", ("groups", "fsdp"), None),
            P("replica", ("groups", "fsdp"), None),
            P("replica", ("groups", "fsdp"), None),
        ),
        check_vma=False,
    )
```

```python
import math

import jax
import jax.numpy as jnp
from jax import lax
from jax.experimental import pallas as pl
from jax.experimental.pallas import tpu as pltpu
from jax.sharding import PartitionSpec as P

norm_eps = 1e-05
logit_cap = 30.0
learn_rate = 0.001
weight_decay = 0.1
beta_one = 0.9
beta_two = 0.999
adam_eps = 1e-08


def shortened(x):
    return jax.tree.map(lambda a: a.astype(jnp.bfloat16) if a.dtype == jnp.float32 else a, x)


def from_partner(block, axis, stride):
    count = lax.axis_size(axis)
    route = []
    for low in range(count):
        high = low | 1 << stride
        if high != low and high < count:
            route += [(low, high), (high, low)]
    return lax.ppermute(block, axis, route)


def normalize(token_block):
    values = token_block.astype(jnp.float32)
    center = values - jnp.mean(values, axis=-1, keepdims=True)
    inv_scale = lax.rsqrt(jnp.mean(center * center, axis=-1, keepdims=True) + norm_eps)
    return (center * inv_scale, inv_scale)


def pair_with(bit_index):

    def swap_values(values):
        return jax.tree.map(
            lambda part, own: part.astype(own.dtype),
            from_partner(shortened(values), "replica", bit_index),
            values,
        )

    return swap_values


def local_any(hidden, targets, params, moment, second, train_step):
    normalized, inv_scale = normalize(hidden[0])
    normed_bf = normalized.astype(jnp.bfloat16)
    labels = targets[0]
    shard_bf = params[0].astype(jnp.bfloat16)
    vocab_width = shard_bf.shape[1]
    weight_bf = lax.all_gather(shard_bf, "fsdp", axis=0, tiled=True)
    raw_logits = jnp.dot(normed_bf, weight_bf, preferred_element_type=jnp.float32)
    capped = jnp.tanh(raw_logits / logit_cap)
    exp_logits = jnp.exp(logit_cap * capped)
    softmax_p = exp_logits / jnp.sum(exp_logits, axis=-1, keepdims=True)
    onehot = (labels[:, None] == jnp.arange(vocab_width, dtype=jnp.int32)[None, :]).astype(
        jnp.float32
    )
    logit_grad = ((softmax_p - onehot) * (1.0 - capped * capped)).astype(jnp.bfloat16)
    full_grad = lax.dot_general(
        normed_bf, logit_grad, (((0,), (0,)), ((), ())), preferred_element_type=jnp.float32
    )
    grad_shard = lax.psum_scatter(
        full_grad.astype(jnp.bfloat16), "fsdp", scatter_dimension=0, tiled=True
    ).astype(jnp.float32)
    normed_grad = lax.dot_general(
        logit_grad, weight_bf, (((1,), (1,)), ((), ())), preferred_element_type=jnp.float32
    )
    first_mean = jnp.mean(normed_grad, axis=-1, keepdims=True)
    second_mean = jnp.mean(normed_grad * normalized, axis=-1, keepdims=True)
    grad_hidden = (inv_scale * (normed_grad - first_mean - normalized * second_mean)).astype(
        jnp.bfloat16
    )
    tcount = train_step[0].astype(jnp.float32)
    fix_one = 1.0 - jnp.exp(tcount * math.log(beta_one))
    fix_two = 1.0 - jnp.exp(tcount * math.log(beta_two))
    replica_grads = grad_shard[None]
    moment_new = beta_one * moment + (1.0 - beta_one) * replica_grads
    second_new = beta_two * second + (1.0 - beta_two) * replica_grads * replica_grads
    adam_step = moment_new / fix_one / (jnp.sqrt(second_new / fix_two) + adam_eps)
    updated = params - learn_rate * (adam_step + weight_decay * params)
    levels = lax.axis_size("replica").bit_length() - 1
    partner_values = lax.switch(
        train_step[0] % levels, [pair_with(bit_index) for bit_index in range(levels)], updated
    )
    averaged = 0.5 * (updated + partner_values)
    return (averaged, moment_new, second_new, grad_hidden[None])


near_route = [(0, 1), (1, 0), (2, 3), (3, 2)]
far_route = [(0, 2), (2, 0), (1, 3), (3, 1)]
chunk_rows = 256

f32 = jnp.float32
bf16 = jnp.bfloat16
vmem = pl.BlockSpec(memory_space=pltpu.VMEM)
smem = pl.BlockSpec(memory_space=pltpu.SMEM)
anywhere = pl.BlockSpec(memory_space=pl.ANY)
dma = pltpu.SemaphoreType.DMA


def shaped(shape, dtype):
    return jax.ShapeDtypeStruct(shape, dtype)


def run(kernel, ins, outs, args, scratch=(), limit=10, flops=0, moved=0, out_specs=None, alias=None):
    if out_specs is None:
        out_specs = [vmem] * len(outs)
    results = pl.pallas_call(
        kernel,
        in_specs=ins,
        out_specs=out_specs,
        out_shape=outs,
        scratch_shapes=list(scratch),
        input_output_aliases=alias or {},
        compiler_params=pltpu.CompilerParams(vmem_limit_bytes=limit << 20),
        cost_estimate=pl.CostEstimate(flops=flops, bytes_accessed=moved, transcendentals=0),
    )(*args)
    return list(results)


def columns(block, width):
    return pl.ds(pl.multiple_of(block * width, 128), width)


def nt_dot(a, b):
    return lax.dot_general(a, b, (((1,), (1,)), ((), ())), preferred_element_type=f32)


def tn_dot(a, b):
    return lax.dot_general(a, b, (((0,), (0,)), ((), ())), preferred_element_type=f32)


def nn_dot(a, b):
    return jnp.dot(a, b, preferred_element_type=f32)


def round_weight_kernel(params_ref, a_ref, b_ref, whole_ref, held_a, held_b, sems):
    rows = held_a.shape[0]
    rest = held_b.shape[0]
    first = pltpu.make_async_copy(params_ref.at[pl.ds(0, rows), 0, :], held_a, sems.at[0])
    later = pltpu.make_async_copy(params_ref.at[pl.ds(rows, rest), 0, :], held_b, sems.at[1])
    first.start()
    later.start()
    first.wait()
    rounded = held_a[...].astype(bf16)
    a_ref[...] = rounded
    whole_ref[0:rows, :] = rounded
    later.wait()
    b_ref[0:rest, :] = held_b[...].astype(bf16)
    b_ref[rest:, :] = jnp.zeros((b_ref.shape[0] - rest, b_ref.shape[1]), bf16)
    whole_ref[rows:, :] = b_ref[...]


def norm_kernel(hidden_ref, normed_ref, mean_ref, inv_ref):
    rows, width = hidden_ref.shape
    depth = normed_ref.shape[2]
    place = lax.axis_index("fsdp")
    step = 128
    for top in range(0, rows, step):
        part = pl.ds(top, step)
        values = hidden_ref[part, :].astype(f32)
        mean = jnp.mean(values, axis=-1, keepdims=True)
        center = values - mean
        inv = lax.rsqrt(jnp.mean(center * center, axis=-1, keepdims=True) + norm_eps)
        mean_ref[part, :] = mean
        inv_ref[part, :] = inv
        for slot in range(normed_ref.shape[0]):
            block = place ^ slot
            own = hidden_ref[part, columns(block, depth)].astype(f32)
            normed_ref[slot, part, :] = ((own - mean) * inv).astype(bf16)


def tiled_kernel(params_ref, moment_ref, second_ref, params_out, moment_out, second_out, sems):
    copies = []
    for slot, (src, dst) in enumerate(
        ((params_ref, params_out), (moment_ref, moment_out), (second_ref, second_out))
    ):
        copies.append(pltpu.make_async_copy(src.at[:, 0, :], dst, sems.at[slot]))
        copies[-1].start()
    for copy in copies:
        copy.wait()


def logits_kernel(own_ref, near_ref, far_a, cross_a, far_b, normed_ref, raw_a_ref, acc_b_ref):
    rows = far_a.shape[0]
    raw = nt_dot(own_ref[0:rows, :], normed_ref[0]) + nt_dot(near_ref[0:rows, :], normed_ref[1])
    raw_a_ref[...] = raw + nt_dot(far_a[...], normed_ref[2]) + nt_dot(cross_a[...], normed_ref[3])
    acc = nt_dot(own_ref[rows:, :], normed_ref[0]) + nt_dot(near_ref[rows:, :], normed_ref[1])
    acc_b_ref[...] = acc + nt_dot(far_b[...], normed_ref[2])


def head_kernel(vocab, raw_a_ref, acc_b_ref, cross_b, normed_ref, labels_ref, lg_a_ref, lg_b_ref, cross_a_ref, cross_b_ref):
    rows = raw_a_ref.shape[0]
    raws = (raw_a_ref[...], acc_b_ref[...] + nt_dot(cross_b[...], normed_ref[3]))
    capped, exps, hots = [], [], []
    for raw, top in zip(raws, (0, rows)):
        capped.append(jnp.tanh(raw / logit_cap))
        ids = lax.broadcasted_iota(jnp.int32, raw.shape, 0) + top
        exp_logits = jnp.exp(logit_cap * capped[-1])
        exps.append(jnp.where(ids < vocab, exp_logits, 0.0) if top else exp_logits)
        hots.append((ids == labels_ref[...]).astype(f32))
    total = sum(jnp.sum(part, axis=0, keepdims=True) for part in exps)
    for cap, part, hot, lg_ref, out_ref in zip(
        capped, exps, hots, (lg_a_ref, lg_b_ref), (cross_a_ref, cross_b_ref)
    ):
        logit_grad = ((part / total - hot) * (1.0 - cap * cap)).astype(bf16)
        lg_ref[...] = logit_grad
        out_ref[...] = nn_dot(logit_grad, normed_ref[3]).astype(bf16)


def grads_kernel(lg_a, lg_b, normed_ref, own_a, own_b, near_a, near_b, far_a, far_b):
    for slot, outs in ((2, (far_a, far_b)), (1, (near_a, near_b)), (0, (own_a, own_b))):
        for lg, out in zip((lg_a, lg_b), outs):
            out[...] = nn_dot(lg[...], normed_ref[slot]).astype(bf16)


def add_kernel(a_ref, b_ref, out_ref):
    out_ref[...] = (a_ref[...].astype(f32) + b_ref[...].astype(f32)).astype(bf16)


def hidden_grad_kernel(lg_a, lg_b, *refs):
    whole, weights_a, weights_b = refs[0:2], refs[2:4], refs[4:6]
    hidden_ref, mean_ref, inv_ref, out_ref, held = refs[6:]
    top = lg_a.shape[0]
    rows, width = hidden_ref.shape
    slots, _, depth = held.shape
    place = lax.axis_index("fsdp")
    mean, inv = mean_ref[...], inv_ref[...]
    first = jnp.zeros((rows, 1), f32)
    second = jnp.zeros((rows, 1), f32)
    for slot in range(slots):
        if slot < 2:
            block_a, block_b = whole[slot][0:top, :], whole[slot][top:, :]
        else:
            block_a, block_b = weights_a[slot - 2][...], weights_b[slot - 2][...]
        back = tn_dot(lg_a[...], block_a) + tn_dot(lg_b[...], block_b)
        held[slot] = back
        normalized = (hidden_ref[:, columns(place ^ slot, depth)].astype(f32) - mean) * inv
        first = first + jnp.sum(back, axis=-1, keepdims=True)
        second = second + jnp.sum(back * normalized, axis=-1, keepdims=True)
    first, second = first / width, second / width
    for slot in range(slots):
        part = columns(place ^ slot, depth)
        normalized = (hidden_ref[:, part].astype(f32) - mean) * inv
        out_ref[:, part] = (inv * (held[slot] - first - normalized * second)).astype(bf16)


def step_kernel(top, count_ref, own_ref, near_ref, far_ref, params_ref, moment_ref, second_ref, *refs):
    if top:
        refs = refs[2:]
    updated_ref, sent_ref, moment_out, second_out, held_moment, held_second, sems = refs
    rows = updated_ref.shape[0]
    part = pl.ds(top, rows)
    target = pl.ds(0, rows)
    grads = sum(ref[target, :].astype(f32) for ref in (own_ref, near_ref, far_ref))
    moment_new = beta_one * moment_ref[part, :] + (1.0 - beta_one) * grads
    held_moment[...] = moment_new
    first = pltpu.make_async_copy(held_moment, moment_out.at[part, 0, :], sems.at[0])
    first.start()
    second_new = beta_two * second_ref[part, :] + (1.0 - beta_two) * grads * grads
    held_second[...] = second_new
    later = pltpu.make_async_copy(held_second, second_out.at[part, 0, :], sems.at[1])
    later.start()
    tcount = jnp.full((1, updated_ref.shape[1]), count_ref[0].astype(f32))
    fix_one = 1.0 / (1.0 - jnp.exp(tcount * math.log(beta_one)))
    fix_two = 1.0 / (1.0 - jnp.exp(tcount * math.log(beta_two)))
    adam_step = moment_new * fix_one / (jnp.sqrt(second_new * fix_two) + adam_eps)
    params = params_ref[part, :]
    updated = params - learn_rate * (adam_step + weight_decay * params)
    updated_ref[...] = updated
    sent_ref[target, :] = updated.astype(bf16)
    rest = sent_ref.shape[0] - rows
    if rest:
        sent_ref[rows:, :] = jnp.zeros((rest, sent_ref.shape[1]), bf16)
    first.wait()
    later.wait()


def average_kernel(top, levels, count_ref, updated_ref, *refs):
    partners = refs[:levels]
    out_ref, held, sem = refs[-3:]
    rows = held.shape[0]
    level = lax.rem(count_ref[0], levels)
    partner = partners[0][0:rows, :]
    for bit in range(1, levels):
        partner = jnp.where(level == bit, partners[bit][0:rows, :], partner)
    held[...] = 0.5 * (updated_ref[...] + partner.astype(f32))
    copy = pltpu.make_async_copy(held, out_ref.at[pl.ds(top, rows), 0, :], sem)
    copy.start()
    copy.wait()


def by_vocab(shard):
    return jnp.transpose(shard, (2, 0, 1))


def local_line(hidden, targets, params, moment, second, train_step):
    tokens, width = hidden.shape[1:]
    depth, vocab = params.shape[1:]
    padded = -(-vocab // 16) * 16
    state_t = [by_vocab(shard) for shard in (params, moment, second)]
    heights = (chunk_rows, padded - chunk_rows)
    tops = (0, chunk_rows)
    counts = (chunk_rows, vocab - chunk_rows)
    shards = [shaped((height, depth), bf16) for height in heights]
    held = [pltpu.VMEM((count, depth), f32) for count in counts]
    state = shaped((vocab, depth), f32)
    state_out = shaped((vocab, 1, depth), f32)
    dot_flops = 2 * padded * tokens * depth

    def hop(block, route):
        return lax.ppermute(block, "fsdp", route)

    whole_shard = shaped((padded, depth), bf16)
    *own, own_whole = run(
        round_weight_kernel, [anywhere], [*shards, whole_shard], (state_t[0],), [*held, dma((2,))]
    )
    far = [hop(block, far_route) for block in own]
    near = hop(own_whole, near_route)
    normed, mean, inv = run(
        norm_kernel,
        [vmem],
        [shaped((4, tokens, depth), bf16), shaped((tokens, 1), f32), shaped((tokens, 1), f32)],
        (hidden[0],),
        flops=10 * tokens * width,
        moved=4 * tokens * width,
    )
    tiled = run(tiled_kernel, [anywhere] * 3, [state] * 3, state_t, [dma((3,))])
    far[0], normed, *tiled = lax.optimization_barrier((far[0], normed, *tiled))
    cross = [hop(block, near_route) for block in far]
    raw_a, acc_b = run(
        logits_kernel,
        [vmem] * 6,
        [shaped((height, tokens), f32) for height in heights],
        (own_whole, near, far[0], cross[0], far[1], normed),
        flops=3 * dot_flops,
    )
    lg_a, lg_b, cross_part_a, cross_part_b = run(
        lambda *refs: head_kernel(vocab, *refs),
        [vmem] * 5,
        [shaped((height, tokens), bf16) for height in heights] + shards,
        (raw_a, acc_b, cross[1], normed, targets),
        flops=2 * dot_flops,
    )
    got_a, got_b = [hop(block, near_route) for block in (cross_part_a, cross_part_b)]
    own_a, own_b, near_a, near_b, far_a, far_b = run(
        grads_kernel, [vmem] * 3, shards * 3, (lg_a, lg_b, normed), flops=3 * dot_flops
    )
    sum_a = run(add_kernel, [vmem] * 2, [shards[0]], (far_a, got_a))[0]
    got_b, near_a, sum_a = lax.optimization_barrier((got_b, near_a, sum_a))
    sum_b = run(add_kernel, [vmem] * 2, [shards[1]], (far_b, got_b))[0]
    near_b, sum_b = lax.optimization_barrier((near_b, sum_b))
    got_far = [hop(block, far_route) for block in (sum_a, sum_b)]
    got_near = [hop(block, near_route) for block in (near_a, near_b)]
    grad_hidden = run(
        hidden_grad_kernel,
        [vmem] * 11,
        [shaped((tokens, width), bf16)],
        (lg_a, lg_b, own_whole, near, far[0], cross[0], far[1], cross[1], hidden[0], mean, inv),
        [pltpu.VMEM((4, tokens, depth), f32)],
        flops=4 * dot_flops,
    )[0]
    got_far[0], grad_hidden = lax.optimization_barrier((got_far[0], grad_hidden))
    levels = lax.axis_size("replica").bit_length() - 1
    updated, partners, moments = [], [], []
    for index, top in enumerate(tops):
        fresh, sent, *moments = run(
            lambda *refs, top=top: step_kernel(top, *refs),
            [smem] + [vmem] * 6 + [anywhere] * len(moments),
            [shaped((counts[index], depth), f32), shards[index], state_out, state_out],
            (train_step, (own_a, own_b)[index], got_near[index], got_far[index], *tiled, *moments),
            [held[index], held[index], dma((2,))],
            out_specs=[vmem, vmem, anywhere, anywhere],
            alias={7: 2, 8: 3} if top else None,
        )
        updated.append(fresh)
        partners.append([from_partner(sent, "replica", bit) for bit in range(levels)])
    partners[0], updated[1] = lax.optimization_barrier((partners[0], updated[1]))
    averaged = []
    for index, top in enumerate(tops):
        averaged = run(
            lambda *refs, top=top: average_kernel(top, levels, *refs),
            [smem] + [vmem] * (1 + levels) + [anywhere] * len(averaged),
            [state_out],
            (train_step, updated[index], *partners[index], *averaged),
            [held[index], dma],
            out_specs=[anywhere],
            alias={2 + levels: 0} if top else None,
        )
    outs = [jnp.transpose(out, (1, 2, 0)) for out in (averaged[0], *moments)]
    return (*outs, grad_hidden[None])


def local(hidden, targets, params, moment, second, train_step):
    four = lax.axis_size("fsdp") == 4 and params.shape[1] % 128 == 0 and hidden.shape[1] % 128 == 0
    four = four and params.shape[2] > chunk_rows
    chosen = local_line if four else local_any
    return chosen(hidden, targets, params, moment, second, train_step)


def solution(mesh):
    placed = (
        P("replica", ("groups", "fsdp"), None),
        P("replica", ("groups", "fsdp")),
        P("replica", ("groups", "fsdp"), None),
        P("replica", ("groups", "fsdp"), None),
        P("replica", ("groups", "fsdp"), None),
        P(),
    )
    return jax.shard_map(
        local,
        mesh=mesh,
        in_specs=placed,
        out_specs=(
            P("replica", ("groups", "fsdp"), None),
            P("replica", ("groups", "fsdp"), None),
            P("replica", ("groups", "fsdp"), None),
            P("replica", ("groups", "fsdp"), None),
        ),
        check_vma=False,
    )
```

```python
import math

import jax
import jax.numpy as jnp
from jax import lax
from jax.experimental import pallas as pl
from jax.experimental.pallas import tpu as pltpu
from jax.sharding import PartitionSpec as P

norm_eps = 1e-05
logit_cap = 30.0
learn_rate = 0.001
weight_decay = 0.1
beta_one = 0.9
beta_two = 0.999
adam_eps = 1e-08


def shortened(x):
    return jax.tree.map(lambda a: a.astype(jnp.bfloat16) if a.dtype == jnp.float32 else a, x)


def from_partner(block, axis, stride):
    count = lax.axis_size(axis)
    route = []
    for low in range(count):
        high = low | 1 << stride
        if high != low and high < count:
            route += [(low, high), (high, low)]
    return lax.ppermute(block, axis, route)


def normalize(token_block):
    values = token_block.astype(jnp.float32)
    center = values - jnp.mean(values, axis=-1, keepdims=True)
    inv_scale = lax.rsqrt(jnp.mean(center * center, axis=-1, keepdims=True) + norm_eps)
    return (center * inv_scale, inv_scale)


def pair_with(bit_index):

    def swap_values(values):
        return jax.tree.map(
            lambda part, own: part.astype(own.dtype),
            from_partner(shortened(values), "replica", bit_index),
            values,
        )

    return swap_values


def local_any(hidden, targets, params, moment, second, train_step):
    normalized, inv_scale = normalize(hidden[0])
    normed_bf = normalized.astype(jnp.bfloat16)
    labels = targets[0]
    shard_bf = params[0].astype(jnp.bfloat16)
    vocab_width = shard_bf.shape[1]
    weight_bf = lax.all_gather(shard_bf, "fsdp", axis=0, tiled=True)
    raw_logits = jnp.dot(normed_bf, weight_bf, preferred_element_type=jnp.float32)
    capped = jnp.tanh(raw_logits / logit_cap)
    exp_logits = jnp.exp(logit_cap * capped)
    softmax_p = exp_logits / jnp.sum(exp_logits, axis=-1, keepdims=True)
    onehot = (labels[:, None] == jnp.arange(vocab_width, dtype=jnp.int32)[None, :]).astype(
        jnp.float32
    )
    logit_grad = ((softmax_p - onehot) * (1.0 - capped * capped)).astype(jnp.bfloat16)
    full_grad = lax.dot_general(
        normed_bf, logit_grad, (((0,), (0,)), ((), ())), preferred_element_type=jnp.float32
    )
    grad_shard = lax.psum_scatter(
        full_grad.astype(jnp.bfloat16), "fsdp", scatter_dimension=0, tiled=True
    ).astype(jnp.float32)
    normed_grad = lax.dot_general(
        logit_grad, weight_bf, (((1,), (1,)), ((), ())), preferred_element_type=jnp.float32
    )
    first_mean = jnp.mean(normed_grad, axis=-1, keepdims=True)
    second_mean = jnp.mean(normed_grad * normalized, axis=-1, keepdims=True)
    grad_hidden = (inv_scale * (normed_grad - first_mean - normalized * second_mean)).astype(
        jnp.bfloat16
    )
    tcount = train_step[0].astype(jnp.float32)
    fix_one = 1.0 - jnp.exp(tcount * math.log(beta_one))
    fix_two = 1.0 - jnp.exp(tcount * math.log(beta_two))
    replica_grads = grad_shard[None]
    moment_new = beta_one * moment + (1.0 - beta_one) * replica_grads
    second_new = beta_two * second + (1.0 - beta_two) * replica_grads * replica_grads
    adam_step = moment_new / fix_one / (jnp.sqrt(second_new / fix_two) + adam_eps)
    updated = params - learn_rate * (adam_step + weight_decay * params)
    levels = lax.axis_size("replica").bit_length() - 1
    partner_values = lax.switch(
        train_step[0] % levels, [pair_with(bit_index) for bit_index in range(levels)], updated
    )
    averaged = 0.5 * (updated + partner_values)
    return (averaged, moment_new, second_new, grad_hidden[None])


near_route = [(0, 1), (1, 0), (2, 3), (3, 2)]
far_route = [(0, 2), (2, 0), (1, 3), (3, 1)]
chunk_rows = 256

f32 = jnp.float32
bf16 = jnp.bfloat16
vmem = pl.BlockSpec(memory_space=pltpu.VMEM)
smem = pl.BlockSpec(memory_space=pltpu.SMEM)
anywhere = pl.BlockSpec(memory_space=pl.ANY)
hbm = pl.BlockSpec(memory_space=pltpu.HBM)
dma = pltpu.SemaphoreType.DMA


def shaped(shape, dtype):
    return jax.ShapeDtypeStruct(shape, dtype)


def run(kernel, ins, outs, args, scratch=(), limit=10, flops=0, moved=0, out_specs=None, alias=None):
    if out_specs is None:
        out_specs = [vmem] * len(outs)
    results = pl.pallas_call(
        kernel,
        in_specs=ins,
        out_specs=out_specs,
        out_shape=outs,
        scratch_shapes=list(scratch),
        input_output_aliases=alias or {},
        compiler_params=pltpu.CompilerParams(vmem_limit_bytes=limit << 20),
        cost_estimate=pl.CostEstimate(flops=flops, bytes_accessed=moved, transcendentals=0),
    )(*args)
    return list(results)


def columns(block, width):
    return pl.ds(pl.multiple_of(block * width, 128), width)


def nt_dot(a, b):
    return lax.dot_general(a, b, (((1,), (1,)), ((), ())), preferred_element_type=f32)


def tn_dot(a, b):
    return lax.dot_general(a, b, (((0,), (0,)), ((), ())), preferred_element_type=f32)


def nn_dot(a, b):
    return jnp.dot(a, b, preferred_element_type=f32)


def fetch(src, top, held, sems):
    rows = held.shape[0]
    pieces = sems.shape[0]
    step = -(-rows // pieces // 8) * 8
    copies = []
    for piece in range(pieces):
        start = piece * step
        count = min(step, rows - start)
        copies.append(
            pltpu.make_async_copy(
                src.at[pl.ds(top + start, count), 0, :], held.at[pl.ds(start, count)], sems.at[piece]
            )
        )
        copies[-1].start()
    for copy in copies:
        copy.wait()


def round_weight_kernel(params_ref, a_ref, b_ref, whole_ref, held, sems):
    rows, total = a_ref.shape[0], held.shape[0]
    rest = total - rows
    fetch(params_ref, 0, held, sems)
    a_ref[...] = held[0:rows, :].astype(bf16)
    b_ref[0:rest, :] = held[rows:, :].astype(bf16)
    b_ref[rest:, :] = jnp.zeros((b_ref.shape[0] - rest, b_ref.shape[1]), bf16)
    whole_ref[0:rows, :] = a_ref[...]
    whole_ref[rows:, :] = b_ref[...]


def norm_kernel(_, hidden_ref, normed_ref, mean_ref, inv_ref):
    rows, width = hidden_ref.shape
    depth = normed_ref.shape[2]
    place = lax.axis_index("fsdp")
    step = 128
    for top in range(0, rows, step):
        part = pl.ds(top, step)
        values = hidden_ref[part, :].astype(f32)
        mean = jnp.mean(values, axis=-1, keepdims=True)
        center = values - mean
        inv = lax.rsqrt(jnp.mean(center * center, axis=-1, keepdims=True) + norm_eps)
        mean_ref[part, :] = mean
        inv_ref[part, :] = inv
        for slot in range(normed_ref.shape[0]):
            block = place ^ slot
            own = hidden_ref[part, columns(block, depth)].astype(f32)
            normed_ref[slot, part, :] = ((own - mean) * inv).astype(bf16)


def tiled_kernel(params_ref, moment_ref, second_ref, params_out, moment_out, second_out, sems):
    copies = []
    for slot, (src, dst) in enumerate(
        ((params_ref, params_out), (moment_ref, moment_out), (second_ref, second_out))
    ):
        copies.append(pltpu.make_async_copy(src.at[:, 0, :], dst, sems.at[slot]))
        copies[-1].start()
    for copy in copies:
        copy.wait()


def logits_kernel(own_ref, near_ref, far_a, cross_a, far_b, normed_ref, raw_a_ref, acc_b_ref):
    rows = far_a.shape[0]
    raw = nt_dot(own_ref[0:rows, :], normed_ref[0]) + nt_dot(near_ref[0:rows, :], normed_ref[1])
    raw_a_ref[...] = raw + nt_dot(far_a[...], normed_ref[2]) + nt_dot(cross_a[...], normed_ref[3])
    acc = nt_dot(own_ref[rows:, :], normed_ref[0]) + nt_dot(near_ref[rows:, :], normed_ref[1])
    acc_b_ref[...] = acc + nt_dot(far_b[...], normed_ref[2])


def head_kernel(vocab, raw_a_ref, acc_b_ref, cross_b, normed_ref, labels_ref, lg_a_ref, lg_b_ref, cross_a_ref, cross_b_ref):
    rows = raw_a_ref.shape[0]
    raws = (raw_a_ref[...], acc_b_ref[...] + nt_dot(cross_b[...], normed_ref[3]))
    capped, exps, hots = [], [], []
    for raw, top in zip(raws, (0, rows)):
        capped.append(jnp.tanh(raw / logit_cap))
        ids = lax.broadcasted_iota(jnp.int32, raw.shape, 0) + top
        exp_logits = jnp.exp(logit_cap * capped[-1])
        exps.append(jnp.where(ids < vocab, exp_logits, 0.0) if top else exp_logits)
        hots.append((ids == labels_ref[...]).astype(f32))
    total = sum(jnp.sum(part, axis=0, keepdims=True) for part in exps)
    for cap, part, hot, lg_ref, out_ref in zip(
        capped, exps, hots, (lg_a_ref, lg_b_ref), (cross_a_ref, cross_b_ref)
    ):
        logit_grad = ((part / total - hot) * (1.0 - cap * cap)).astype(bf16)
        lg_ref[...] = logit_grad
        out_ref[...] = nn_dot(logit_grad, normed_ref[3]).astype(bf16)


def grads_kernel(lg_a, lg_b, normed_ref, own_a, own_b, near_a, near_b, far_a, far_b):
    for slot, outs in ((2, (far_a, far_b)), (1, (near_a, near_b)), (0, (own_a, own_b))):
        for lg, out in zip((lg_a, lg_b), outs):
            out[...] = nn_dot(lg[...], normed_ref[slot]).astype(bf16)


def add_kernel(a_ref, b_ref, out_ref):
    out_ref[...] = (a_ref[...].astype(f32) + b_ref[...].astype(f32)).astype(bf16)


def hidden_grad_kernel(lg_a, lg_b, *refs):
    whole, weights_a, weights_b = refs[0:2], refs[2:4], refs[4:6]
    hidden_ref, mean_ref, inv_ref, out_ref, held = refs[6:]
    top = lg_a.shape[0]
    rows, width = hidden_ref.shape
    slots, _, depth = held.shape
    place = lax.axis_index("fsdp")
    mean, inv = mean_ref[...], inv_ref[...]
    first = jnp.zeros((rows, 1), f32)
    second = jnp.zeros((rows, 1), f32)
    for slot in range(slots):
        if slot < 2:
            block_a, block_b = whole[slot][0:top, :], whole[slot][top:, :]
        else:
            block_a, block_b = weights_a[slot - 2][...], weights_b[slot - 2][...]
        back = tn_dot(lg_a[...], block_a) + tn_dot(lg_b[...], block_b)
        held[slot] = back
        normalized = (hidden_ref[:, columns(place ^ slot, depth)].astype(f32) - mean) * inv
        first = first + jnp.sum(back, axis=-1, keepdims=True)
        second = second + jnp.sum(back * normalized, axis=-1, keepdims=True)
    first, second = first / width, second / width
    for slot in range(slots):
        part = columns(place ^ slot, depth)
        normalized = (hidden_ref[:, part].astype(f32) - mean) * inv
        out_ref[:, part] = (inv * (held[slot] - first - normalized * second)).astype(bf16)


def step_kernel(top, count_ref, own_ref, near_ref, far_ref, params_ref, moment_ref, second_ref,
                updated_ref, sent_ref, moment_out, second_out):
    rows = updated_ref.shape[0]
    part = pl.ds(top, rows)
    target = pl.ds(0, rows)
    grads = sum(ref[target, :].astype(f32) for ref in (own_ref, near_ref, far_ref))
    moment_new = beta_one * moment_ref[part, :] + (1.0 - beta_one) * grads
    second_new = beta_two * second_ref[part, :] + (1.0 - beta_two) * grads * grads
    moment_out[...] = moment_new
    second_out[...] = second_new
    tcount = jnp.full((1, updated_ref.shape[1]), count_ref[0].astype(f32))
    fix_one = 1.0 / (1.0 - jnp.exp(tcount * math.log(beta_one)))
    fix_two = 1.0 / (1.0 - jnp.exp(tcount * math.log(beta_two)))
    adam_step = moment_new * fix_one / (jnp.sqrt(second_new * fix_two) + adam_eps)
    params = params_ref[part, :]
    updated = params - learn_rate * (adam_step + weight_decay * params)
    updated_ref[...] = updated
    sent_ref[target, :] = updated.astype(bf16)
    rest = sent_ref.shape[0] - rows
    if rest:
        sent_ref[rows:, :] = jnp.zeros((rest, sent_ref.shape[1]), bf16)


def store_kernel(top, moment_ref, second_ref, *refs):
    moment_out, second_out, sems = refs[-3:]
    part = pl.ds(top, moment_ref.shape[0])
    copies = [
        pltpu.make_async_copy(moment_ref, moment_out.at[part, 0, :], sems.at[0]),
        pltpu.make_async_copy(second_ref, second_out.at[part, 0, :], sems.at[1]),
    ]
    for copy in copies:
        copy.start()
    for copy in copies:
        copy.wait()


def average_kernel(top, levels, count_ref, updated_ref, *refs):
    partners = refs[:levels]
    out_ref, held, sem = refs[-3:]
    rows = held.shape[0]
    level = lax.rem(count_ref[0], levels)
    partner = partners[0][0:rows, :]
    for bit in range(1, levels):
        partner = jnp.where(level == bit, partners[bit][0:rows, :], partner)
    held[...] = 0.5 * (updated_ref[...] + partner.astype(f32))
    copy = pltpu.make_async_copy(held, out_ref.at[pl.ds(top, rows), 0, :], sem)
    copy.start()
    copy.wait()


def by_vocab(shard):
    return jnp.transpose(shard, (2, 0, 1))


def local_line(hidden, targets, params, moment, second, train_step):
    tokens, width = hidden.shape[1:]
    depth, vocab = params.shape[1:]
    padded = -(-vocab // 16) * 16
    state_t = [by_vocab(shard) for shard in (params, moment, second)]
    heights = (chunk_rows, padded - chunk_rows)
    tops = (0, chunk_rows)
    counts = (chunk_rows, vocab - chunk_rows)
    shards = [shaped((height, depth), bf16) for height in heights]
    held = [pltpu.VMEM((count, depth), f32) for count in counts]
    state = shaped((vocab, depth), f32)
    state_out = shaped((vocab, 1, depth), f32)
    dot_flops = 2 * padded * tokens * depth

    def hop(block, route):
        return lax.ppermute(block, "fsdp", route)

    whole_shard = shaped((padded, depth), bf16)
    *own, own_whole = run(
        round_weight_kernel,
        [hbm],
        [*shards, whole_shard],
        (state_t[0],),
        [pltpu.VMEM((vocab, depth), f32), dma((4,))],
    )
    far = [hop(block, far_route) for block in own]
    near = hop(own_whole, near_route)
    normed, mean, inv = run(
        norm_kernel,
        [smem, vmem],
        [shaped((4, tokens, depth), bf16), shaped((tokens, 1), f32), shaped((tokens, 1), f32)],
        (train_step, hidden[0]),
        flops=10 * tokens * width,
        moved=4 * tokens * width,
    )
    tiled = run(tiled_kernel, [hbm] * 3, [state] * 3, state_t, [dma((3,))])
    far[0], normed, *tiled = lax.optimization_barrier((far[0], normed, *tiled))
    cross = [hop(block, near_route) for block in far]
    raw_a, acc_b = run(
        logits_kernel,
        [vmem] * 6,
        [shaped((height, tokens), f32) for height in heights],
        (own_whole, near, far[0], cross[0], far[1], normed),
        flops=3 * dot_flops,
    )
    lg_a, lg_b, cross_part_a, cross_part_b = run(
        lambda *refs: head_kernel(vocab, *refs),
        [vmem] * 5,
        [shaped((height, tokens), bf16) for height in heights] + shards,
        (raw_a, acc_b, cross[1], normed, targets),
        flops=2 * dot_flops,
    )
    got_a, got_b = [hop(block, near_route) for block in (cross_part_a, cross_part_b)]
    own_a, own_b, near_a, near_b, far_a, far_b = run(
        grads_kernel, [vmem] * 3, shards * 3, (lg_a, lg_b, normed), flops=3 * dot_flops
    )
    sum_a = run(add_kernel, [vmem] * 2, [shards[0]], (far_a, got_a))[0]
    near_a, later_a = lax.optimization_barrier((near_a, sum_a))
    got_far_a, got_near_a = hop(sum_a, far_route), hop(near_a, near_route)
    got_b, later_a = lax.optimization_barrier((got_b, later_a))
    sum_b = run(add_kernel, [vmem] * 2, [shards[1]], (far_b, got_b))[0]
    lg_late, sum_b = lax.optimization_barrier((lg_a, sum_b))
    grad_hidden = run(
        hidden_grad_kernel,
        [vmem] * 11,
        [shaped((tokens, width), bf16)],
        (lg_late, lg_b, own_whole, near, far[0], cross[0], far[1], cross[1], hidden[0], mean, inv),
        [pltpu.VMEM((4, tokens, depth), f32)],
        flops=4 * dot_flops,
    )[0]
    got_far_a, got_near_a, sum_b, near_b, grad_hidden = lax.optimization_barrier(
        (got_far_a, got_near_a, sum_b, near_b, grad_hidden)
    )
    got_far = [got_far_a, hop(sum_b, far_route)]
    got_near = [got_near_a, hop(near_b, near_route)]
    levels = lax.axis_size("replica").bit_length() - 1
    updated, partners, moments = [], [], []
    for index, top in enumerate(tops):
        state_part = shaped((counts[index], depth), f32)
        fresh, sent, *state_new = run(
            lambda *refs, top=top: step_kernel(top, *refs),
            [smem] + [vmem] * 6,
            [state_part, shards[index], state_part, state_part],
            (train_step, (own_a, own_b)[index], got_near[index], got_far[index], *tiled),
        )
        updated.append(fresh)
        partners.append([from_partner(sent, "replica", bit) for bit in range(levels)])
        moments = run(
            lambda *refs, top=top: store_kernel(top, *refs),
            [vmem] * 2 + [anywhere] * len(moments),
            [state_out] * 2,
            (*state_new, *moments),
            [dma((2,))],
            out_specs=[anywhere] * 2,
            alias={2: 0, 3: 1} if top else None,
        )
    partners[0], updated[1] = lax.optimization_barrier((partners[0], updated[1]))
    averaged = []
    for index, top in enumerate(tops):
        averaged = run(
            lambda *refs, top=top: average_kernel(top, levels, *refs),
            [smem] + [vmem] * (1 + levels) + [anywhere] * len(averaged),
            [state_out],
            (train_step, updated[index], *partners[index], *averaged),
            [held[index], dma],
            out_specs=[anywhere],
            alias={2 + levels: 0} if top else None,
        )
    outs = [jnp.transpose(out, (1, 2, 0)) for out in (averaged[0], *moments)]
    return (*outs, grad_hidden[None])


def local(hidden, targets, params, moment, second, train_step):
    four = lax.axis_size("fsdp") == 4 and params.shape[1] % 128 == 0 and hidden.shape[1] % 128 == 0
    four = four and params.shape[2] > chunk_rows
    chosen = local_line if four else local_any
    return chosen(hidden, targets, params, moment, second, train_step)


def solution(mesh):
    placed = (
        P("replica", ("groups", "fsdp"), None),
        P("replica", ("groups", "fsdp")),
        P("replica", ("groups", "fsdp"), None),
        P("replica", ("groups", "fsdp"), None),
        P("replica", ("groups", "fsdp"), None),
        P(),
    )
    return jax.shard_map(
        local,
        mesh=mesh,
        in_specs=placed,
        out_specs=(
            P("replica", ("groups", "fsdp"), None),
            P("replica", ("groups", "fsdp"), None),
            P("replica", ("groups", "fsdp"), None),
            P("replica", ("groups", "fsdp"), None),
        ),
        check_vma=False,
    )
```

```python
import functools
import math

import jax
import jax.numpy as jnp
from jax import lax
from jax.experimental import pallas as pl
from jax.experimental.pallas import tpu as pltpu
from jax.sharding import PartitionSpec as P

norm_eps = 1e-05
logit_cap = 30.0
learn_rate = 0.001
weight_decay = 0.1
beta_one = 0.9
beta_two = 0.999
adam_eps = 1e-08


def shortened(x):
    return jax.tree.map(lambda a: a.astype(jnp.bfloat16) if a.dtype == jnp.float32 else a, x)


def from_partner(block, axis, stride):
    count = lax.axis_size(axis)
    route = []
    for low in range(count):
        high = low | 1 << stride
        if high != low and high < count:
            route += [(low, high), (high, low)]
    return lax.ppermute(block, axis, route)


def normalize(token_block):
    values = token_block.astype(jnp.float32)
    center = values - jnp.mean(values, axis=-1, keepdims=True)
    inv_scale = lax.rsqrt(jnp.mean(center * center, axis=-1, keepdims=True) + norm_eps)
    return (center * inv_scale, inv_scale)


def pair_with(bit_index):

    def swap_values(values):
        return jax.tree.map(
            lambda part, own: part.astype(own.dtype),
            from_partner(shortened(values), "replica", bit_index),
            values,
        )

    return swap_values


def local_any(hidden, targets, params, moment, second, train_step):
    normalized, inv_scale = normalize(hidden[0])
    normed_bf = normalized.astype(jnp.bfloat16)
    labels = targets[0]
    shard_bf = params[0].astype(jnp.bfloat16)
    vocab_width = shard_bf.shape[1]
    weight_bf = lax.all_gather(shard_bf, "fsdp", axis=0, tiled=True)
    raw_logits = jnp.dot(normed_bf, weight_bf, preferred_element_type=jnp.float32)
    capped = jnp.tanh(raw_logits / logit_cap)
    exp_logits = jnp.exp(logit_cap * capped)
    softmax_p = exp_logits / jnp.sum(exp_logits, axis=-1, keepdims=True)
    onehot = (labels[:, None] == jnp.arange(vocab_width, dtype=jnp.int32)[None, :]).astype(
        jnp.float32
    )
    logit_grad = ((softmax_p - onehot) * (1.0 - capped * capped)).astype(jnp.bfloat16)
    full_grad = lax.dot_general(
        normed_bf, logit_grad, (((0,), (0,)), ((), ())), preferred_element_type=jnp.float32
    )
    grad_shard = lax.psum_scatter(
        full_grad.astype(jnp.bfloat16), "fsdp", scatter_dimension=0, tiled=True
    ).astype(jnp.float32)
    normed_grad = lax.dot_general(
        logit_grad, weight_bf, (((1,), (1,)), ((), ())), preferred_element_type=jnp.float32
    )
    first_mean = jnp.mean(normed_grad, axis=-1, keepdims=True)
    second_mean = jnp.mean(normed_grad * normalized, axis=-1, keepdims=True)
    grad_hidden = (inv_scale * (normed_grad - first_mean - normalized * second_mean)).astype(
        jnp.bfloat16
    )
    tcount = train_step[0].astype(jnp.float32)
    fix_one = 1.0 - jnp.exp(tcount * math.log(beta_one))
    fix_two = 1.0 - jnp.exp(tcount * math.log(beta_two))
    replica_grads = grad_shard[None]
    moment_new = beta_one * moment + (1.0 - beta_one) * replica_grads
    second_new = beta_two * second + (1.0 - beta_two) * replica_grads * replica_grads
    adam_step = moment_new / fix_one / (jnp.sqrt(second_new / fix_two) + adam_eps)
    updated = params - learn_rate * (adam_step + weight_decay * params)
    levels = lax.axis_size("replica").bit_length() - 1
    partner_values = lax.switch(
        train_step[0] % levels, [pair_with(bit_index) for bit_index in range(levels)], updated
    )
    averaged = 0.5 * (updated + partner_values)
    return (averaged, moment_new, second_new, grad_hidden[None])


near_route = [(0, 1), (1, 0), (2, 3), (3, 2)]
far_route = [(0, 2), (2, 0), (1, 3), (3, 1)]
chunk_rows = 256

f32 = jnp.float32
bf16 = jnp.bfloat16
vmem = pl.BlockSpec(memory_space=pltpu.VMEM)
smem = pl.BlockSpec(memory_space=pltpu.SMEM)
hbm = pl.BlockSpec(memory_space=pltpu.HBM)
dma = pltpu.SemaphoreType.DMA


def shaped(shape, dtype):
    return jax.ShapeDtypeStruct(shape, dtype)


def run(kernel, ins, outs, args, scratch=(), limit=10, flops=0, moved=0, out_specs=None, alias=None):
    if out_specs is None:
        out_specs = [vmem] * len(outs)
    results = pl.pallas_call(
        kernel,
        in_specs=ins,
        out_specs=out_specs,
        out_shape=outs,
        scratch_shapes=list(scratch),
        input_output_aliases=alias or {},
        compiler_params=pltpu.CompilerParams(vmem_limit_bytes=limit << 20),
        cost_estimate=pl.CostEstimate(flops=flops, bytes_accessed=moved, transcendentals=0),
    )(*args)
    return list(results)


def columns(block, width):
    return pl.ds(pl.multiple_of(block * width, 128), width)


def nt_dot(a, b):
    return lax.dot_general(a, b, (((1,), (1,)), ((), ())), preferred_element_type=f32)


def tn_dot(a, b):
    return lax.dot_general(a, b, (((0,), (0,)), ((), ())), preferred_element_type=f32)


def nn_dot(a, b):
    return jnp.dot(a, b, preferred_element_type=f32)


def fetch(src, top, held, sems):
    rows = held.shape[0]
    pieces = sems.shape[0]
    step = -(-rows // pieces // 8) * 8
    copies = []
    for piece in range(pieces):
        start = piece * step
        count = min(step, rows - start)
        copies.append(
            pltpu.make_async_copy(
                src.at[pl.ds(top + start, count), 0, :], held.at[pl.ds(start, count)], sems.at[piece]
            )
        )
        copies[-1].start()
    for copy in copies:
        copy.wait()


def round_weight_kernel(params_ref, a_ref, b_ref, whole_ref, held, sems):
    rows, total = a_ref.shape[0], held.shape[0]
    rest = total - rows
    fetch(params_ref, 0, held, sems)
    a_ref[...] = held[0:rows, :].astype(bf16)
    b_ref[0:rest, :] = held[rows:, :].astype(bf16)
    b_ref[rest:, :] = jnp.zeros((b_ref.shape[0] - rest, b_ref.shape[1]), bf16)
    whole_ref[0:rows, :] = a_ref[...]
    whole_ref[rows:, :] = b_ref[...]


def norm_kernel(count_ref, hidden_ref, normed_ref, mean_ref, inv_ref, fix_ref):
    tcount = jnp.full((1, fix_ref.shape[1]), count_ref[0].astype(f32))
    fix_ref[0:1, :] = 1.0 / (1.0 - jnp.exp(tcount * math.log(beta_one)))
    fix_ref[1:2, :] = 1.0 / (1.0 - jnp.exp(tcount * math.log(beta_two)))
    rows, width = hidden_ref.shape
    depth = normed_ref.shape[2]
    place = lax.axis_index("fsdp")
    step = 128
    for top in range(0, rows, step):
        part = pl.ds(top, step)
        values = hidden_ref[part, :].astype(f32)
        mean = jnp.mean(values, axis=-1, keepdims=True)
        center = values - mean
        inv = lax.rsqrt(jnp.mean(center * center, axis=-1, keepdims=True) + norm_eps)
        mean_ref[part, :] = mean
        inv_ref[part, :] = inv
        for slot in range(normed_ref.shape[0]):
            block = place ^ slot
            own = hidden_ref[part, columns(block, depth)].astype(f32)
            normed_ref[slot, part, :] = ((own - mean) * inv).astype(bf16)


def tiled_kernel(params_ref, moment_ref, second_ref, params_out, moment_out, second_out, sems):
    copies = []
    for slot, (src, dst) in enumerate(
        ((params_ref, params_out), (moment_ref, moment_out), (second_ref, second_out))
    ):
        copies.append(pltpu.make_async_copy(src.at[:, 0, :], dst, sems.at[slot]))
        copies[-1].start()
    for copy in copies:
        copy.wait()


def logits_kernel(own_ref, near_ref, far_a, cross_a, far_b, normed_ref, raw_a_ref, acc_b_ref):
    rows = far_a.shape[0]
    raw = nt_dot(own_ref[0:rows, :], normed_ref[0]) + nt_dot(near_ref[0:rows, :], normed_ref[1])
    raw_a_ref[...] = raw + nt_dot(far_a[...], normed_ref[2]) + nt_dot(cross_a[...], normed_ref[3])
    acc = nt_dot(own_ref[rows:, :], normed_ref[0]) + nt_dot(near_ref[rows:, :], normed_ref[1])
    acc_b_ref[...] = acc + nt_dot(far_b[...], normed_ref[2])


def head_kernel(vocab, raw_a_ref, acc_b_ref, cross_b, normed_ref, labels_ref, lg_a_ref, lg_b_ref, cross_a_ref, cross_b_ref):
    rows = raw_a_ref.shape[0]
    raws = (raw_a_ref[...], acc_b_ref[...] + nt_dot(cross_b[...], normed_ref[3]))
    capped, exps, hots = [], [], []
    for raw, top in zip(raws, (0, rows)):
        capped.append(jnp.tanh(raw / logit_cap))
        ids = lax.broadcasted_iota(jnp.int32, raw.shape, 0) + top
        exp_logits = jnp.exp(logit_cap * capped[-1])
        exps.append(jnp.where(ids < vocab, exp_logits, 0.0) if top else exp_logits)
        hots.append((ids == labels_ref[...]).astype(f32))
    total = sum(jnp.sum(part, axis=0, keepdims=True) for part in exps)
    for cap, part, hot, lg_ref, out_ref in zip(
        capped, exps, hots, (lg_a_ref, lg_b_ref), (cross_a_ref, cross_b_ref)
    ):
        logit_grad = ((part / total - hot) * (1.0 - cap * cap)).astype(bf16)
        lg_ref[...] = logit_grad
        out_ref[...] = nn_dot(logit_grad, normed_ref[3]).astype(bf16)


def grads_kernel(lg_a, lg_b, normed_ref, own_a, own_b, near_a, near_b, far_a, far_b):
    for slot, outs in ((2, (far_a, far_b)), (1, (near_a, near_b)), (0, (own_a, own_b))):
        for lg, out in zip((lg_a, lg_b), outs):
            out[...] = nn_dot(lg[...], normed_ref[slot]).astype(bf16)


def add_kernel(a_ref, b_ref, out_ref):
    out_ref[...] = (a_ref[...].astype(f32) + b_ref[...].astype(f32)).astype(bf16)


def hidden_grad_kernel(lg_a, lg_b, *refs):
    whole, weights_a, weights_b = refs[0:2], refs[2:4], refs[4:6]
    hidden_ref, mean_ref, inv_ref, out_ref, held = refs[6:]
    top = lg_a.shape[0]
    rows, width = hidden_ref.shape
    slots, _, depth = held.shape
    place = lax.axis_index("fsdp")
    mean, inv = mean_ref[...], inv_ref[...]
    first = jnp.zeros((rows, 1), f32)
    second = jnp.zeros((rows, 1), f32)
    for slot in range(slots):
        if slot < 2:
            block_a, block_b = whole[slot][0:top, :], whole[slot][top:, :]
        else:
            block_a, block_b = weights_a[slot - 2][...], weights_b[slot - 2][...]
        back = tn_dot(lg_a[...], block_a) + tn_dot(lg_b[...], block_b)
        held[slot] = back
        normalized = (hidden_ref[:, columns(place ^ slot, depth)].astype(f32) - mean) * inv
        first = first + jnp.sum(back, axis=-1, keepdims=True)
        second = second + jnp.sum(back * normalized, axis=-1, keepdims=True)
    first, second = first / width, second / width
    for slot in range(slots):
        part = columns(place ^ slot, depth)
        normalized = (hidden_ref[:, part].astype(f32) - mean) * inv
        out_ref[:, part] = (inv * (held[slot] - first - normalized * second)).astype(bf16)


def step_kernel(top, fix_ref, own_ref, near_ref, far_ref, params_ref, moment_ref, second_ref,
                updated_ref, sent_ref, moment_out, second_out):
    rows = updated_ref.shape[0]
    part = pl.ds(top, rows)
    target = pl.ds(0, rows)
    grads = sum(ref[target, :].astype(f32) for ref in (own_ref, near_ref, far_ref))
    moment_new = beta_one * moment_ref[part, :] + (1.0 - beta_one) * grads
    second_new = beta_two * second_ref[part, :] + (1.0 - beta_two) * grads * grads
    moment_out[...] = moment_new
    second_out[...] = second_new
    fix_one, fix_two = fix_ref[0:1, :], fix_ref[1:2, :]
    adam_step = moment_new * fix_one / (jnp.sqrt(second_new * fix_two) + adam_eps)
    params = params_ref[part, :]
    updated = params - learn_rate * (adam_step + weight_decay * params)
    updated_ref[...] = updated
    sent_ref[target, :] = updated.astype(bf16)
    rest = sent_ref.shape[0] - rows
    if rest:
        sent_ref[rows:, :] = jnp.zeros((rest, sent_ref.shape[1]), bf16)


def send_out(top, pairs, sems):
    copies = [
        pltpu.make_async_copy(source, target.at[pl.ds(top, source.shape[0]), 0, :], sems.at[slot])
        for slot, (source, target) in enumerate(pairs)
    ]
    for copy in copies:
        copy.start()
    return copies


def step_store_kernel(top, *refs):
    *ins, updated_ref, sent_ref, moment_out, second_out, held_moment, held_second, sems = refs
    step_kernel(top, *ins, updated_ref, sent_ref, held_moment, held_second)
    for copy in send_out(top, ((held_moment, moment_out), (held_second, second_out)), sems):
        copy.wait()


def store_kernel(top, moment_ref, second_ref, *refs):
    moment_out, second_out, sems = refs[-3:]
    for copy in send_out(top, ((moment_ref, moment_out), (second_ref, second_out)), sems):
        copy.wait()


def average_kernel(top, updated_ref, partner_ref, *refs):
    out_ref, held, sems = refs[-3:]
    rows = held.shape[0]
    held[...] = 0.5 * (updated_ref[...] + partner_ref[0:rows, :].astype(f32))
    for copy in send_out(top, ((held, out_ref),), sems):
        copy.wait()


def finish_kernel(top, moment_ref, second_ref, updated_ref, partner_ref, *refs):
    moment_out, second_out, out_ref, held, sems = refs[-5:]
    rows = held.shape[0]
    stores = send_out(top, ((moment_ref, moment_out), (second_ref, second_out)), sems)
    held[...] = 0.5 * (updated_ref[...] + partner_ref[0:rows, :].astype(f32))
    copy = pltpu.make_async_copy(held, out_ref.at[pl.ds(top, rows), 0, :], sems.at[2])
    copy.start()
    for each in (*stores, copy):
        each.wait()


def by_vocab(shard):
    return jnp.transpose(shard, (2, 0, 1))


def line_step(bit, hidden, targets, params, moment, second, train_step):
    tokens, width = hidden.shape[1:]
    depth, vocab = params.shape[1:]
    padded = -(-vocab // 16) * 16
    state_t = [by_vocab(shard) for shard in (params, moment, second)]
    heights = (chunk_rows, padded - chunk_rows)
    tops = (0, chunk_rows)
    counts = (chunk_rows, vocab - chunk_rows)
    shards = [shaped((height, depth), bf16) for height in heights]
    held = [pltpu.VMEM((count, depth), f32) for count in counts]
    state = shaped((vocab, depth), f32)
    state_out = pltpu.HBM((vocab, 1, depth), f32)
    dot_flops = 2 * padded * tokens * depth

    def hop(block, route):
        return lax.ppermute(block, "fsdp", route)

    whole_shard = shaped((padded, depth), bf16)
    *own, own_whole = run(
        round_weight_kernel,
        [hbm],
        [*shards, whole_shard],
        (state_t[0],),
        [pltpu.VMEM((vocab, depth), f32), dma((4,))],
    )
    far = [hop(block, far_route) for block in own]
    near = hop(own_whole, near_route)
    normed, mean, inv, fix = run(
        norm_kernel,
        [smem, vmem],
        [shaped((4, tokens, depth), bf16), shaped((tokens, 1), f32), shaped((tokens, 1), f32), shaped((2, depth), f32)],
        (train_step, hidden[0]),
        flops=10 * tokens * width,
        moved=4 * tokens * width,
    )
    tiled = run(tiled_kernel, [hbm] * 3, [state] * 3, state_t, [dma((3,))])
    far[0], normed, *tiled = lax.optimization_barrier((far[0], normed, *tiled))
    cross = [hop(block, near_route) for block in far]
    raw_a, acc_b = run(
        logits_kernel,
        [vmem] * 6,
        [shaped((height, tokens), f32) for height in heights],
        (own_whole, near, far[0], cross[0], far[1], normed),
        flops=3 * dot_flops,
    )
    lg_a, lg_b, cross_part_a, cross_part_b = run(
        lambda *refs: head_kernel(vocab, *refs),
        [vmem] * 5,
        [shaped((height, tokens), bf16) for height in heights] + shards,
        (raw_a, acc_b, cross[1], normed, targets),
        flops=2 * dot_flops,
    )
    got_a, got_b = [hop(block, near_route) for block in (cross_part_a, cross_part_b)]
    own_a, own_b, near_a, near_b, far_a, far_b = run(
        grads_kernel, [vmem] * 3, shards * 3, (lg_a, lg_b, normed), flops=3 * dot_flops
    )
    sum_a = run(add_kernel, [vmem] * 2, [shards[0]], (far_a, got_a))[0]
    near_a, later_a = lax.optimization_barrier((near_a, sum_a))
    got_far_a, got_near_a = hop(sum_a, far_route), hop(near_a, near_route)
    got_b, later_a = lax.optimization_barrier((got_b, later_a))
    sum_b = run(add_kernel, [vmem] * 2, [shards[1]], (far_b, got_b))[0]
    lg_late, sum_b = lax.optimization_barrier((lg_a, sum_b))
    grad_hidden = run(
        hidden_grad_kernel,
        [vmem] * 11,
        [shaped((tokens, width), bf16)],
        (lg_late, lg_b, own_whole, near, far[0], cross[0], far[1], cross[1], hidden[0], mean, inv),
        [pltpu.VMEM((4, tokens, depth), f32)],
        flops=4 * dot_flops,
    )[0]
    if bit:
        got_far_a, got_near_a, sum_b, near_b, grad_hidden = lax.optimization_barrier(
            (got_far_a, got_near_a, sum_b, near_b, grad_hidden)
        )
    else:
        got_far_a, grad_hidden = lax.optimization_barrier((got_far_a, grad_hidden))
    got_far = [got_far_a, hop(sum_b, far_route)]
    got_near = [got_near_a, hop(near_b, near_route)]
    moments, averaged = [], []

    def step(index, kernel, state_new, scratch=()):
        updated, sent, *state_new = run(
            functools.partial(kernel, tops[index]),
            [vmem] * 7,
            [shaped((counts[index], depth), f32), shards[index], *state_new],
            (fix, (own_a, own_b)[index], got_near[index], got_far[index], *tiled),
            scratch,
            out_specs=[vmem, vmem] + [hbm if scratch else vmem] * 2,
        )
        return updated, from_partner(sent, "replica", bit), state_new

    def store(index, state_new, moments):
        return run(
            functools.partial(store_kernel, tops[index]),
            [vmem] * 2 + [hbm] * len(moments),
            [state_out] * 2,
            (*state_new, *moments),
            [dma((2,))],
            out_specs=[hbm] * 2,
            alias={2: 0, 3: 1} if moments else None,
        )

    def average(index, updated, partner, averaged):
        return run(
            functools.partial(average_kernel, tops[index]),
            [vmem] * 2 + [hbm] * len(averaged),
            [state_out],
            (updated, partner, *averaged),
            [held[index], dma((1,))],
            out_specs=[hbm],
            alias={2: 0} if averaged else None,
        )

    state_part = [[shaped((count, depth), f32)] * 2 for count in counts]
    if bit:
        updated_a, partner_a, state_a = step(0, step_kernel, state_part[0])
    else:
        scratch = [held[0], held[0], dma((2,))]
        updated_a, partner_a, moments = step(0, step_store_kernel, [state_out] * 2, scratch)
    updated_b, partner_b, state_b = step(1, step_kernel, state_part[1])
    partner_a, updated_b = lax.optimization_barrier((partner_a, updated_b))
    averaged = average(0, updated_a, partner_a, averaged)
    if bit:
        moments = store(0, state_a, moments)
        moments = store(1, state_b, moments)
        averaged = average(1, updated_b, partner_b, averaged)
    else:
        *moments, averaged[0] = run(
            functools.partial(finish_kernel, tops[1]),
            [vmem] * 4 + [hbm] * 3,
            [state_out] * 3,
            (*state_b, updated_b, partner_b, *moments, *averaged),
            [held[1], dma((3,))],
            out_specs=[hbm] * 3,
            alias={4: 0, 5: 1, 6: 2},
        )
    outs = [jnp.transpose(out, (1, 2, 0)) for out in (averaged[0], *moments)]
    return (*outs, grad_hidden[None])


def local_line(hidden, targets, params, moment, second, train_step):
    levels = lax.axis_size("replica").bit_length() - 1
    branches = [functools.partial(line_step, bit) for bit in range(levels)]
    level = lax.rem(train_step[0], levels)
    return lax.switch(level, branches, hidden, targets, params, moment, second, train_step)


def local(hidden, targets, params, moment, second, train_step):
    four = lax.axis_size("fsdp") == 4 and params.shape[1] % 128 == 0 and hidden.shape[1] % 128 == 0
    four = four and params.shape[2] > chunk_rows
    chosen = local_line if four else local_any
    return chosen(hidden, targets, params, moment, second, train_step)


def solution(mesh):
    placed = (
        P("replica", ("groups", "fsdp"), None),
        P("replica", ("groups", "fsdp")),
        P("replica", ("groups", "fsdp"), None),
        P("replica", ("groups", "fsdp"), None),
        P("replica", ("groups", "fsdp"), None),
        P(),
    )
    return jax.shard_map(
        local,
        mesh=mesh,
        in_specs=placed,
        out_specs=(
            P("replica", ("groups", "fsdp"), None),
            P("replica", ("groups", "fsdp"), None),
            P("replica", ("groups", "fsdp"), None),
            P("replica", ("groups", "fsdp"), None),
        ),
        check_vma=False,
    )
```

```python
import functools
import math

import jax
import jax.numpy as jnp
from jax import lax
from jax.experimental import pallas as pl
from jax.experimental.pallas import tpu as pltpu
from jax.sharding import PartitionSpec as P

norm_eps = 1e-05
logit_cap = 30.0
learn_rate = 0.001
weight_decay = 0.1
beta_one = 0.9
beta_two = 0.999
adam_eps = 1e-08


def shortened(x):
    return jax.tree.map(lambda a: a.astype(jnp.bfloat16) if a.dtype == jnp.float32 else a, x)


def from_partner(block, axis, stride):
    count = lax.axis_size(axis)
    route = []
    for low in range(count):
        high = low | 1 << stride
        if high != low and high < count:
            route += [(low, high), (high, low)]
    return lax.ppermute(block, axis, route)


def normalize(token_block):
    values = token_block.astype(jnp.float32)
    center = values - jnp.mean(values, axis=-1, keepdims=True)
    inv_scale = lax.rsqrt(jnp.mean(center * center, axis=-1, keepdims=True) + norm_eps)
    return (center * inv_scale, inv_scale)


def pair_with(bit_index):

    def swap_values(values):
        return jax.tree.map(
            lambda part, own: part.astype(own.dtype),
            from_partner(shortened(values), "replica", bit_index),
            values,
        )

    return swap_values


def local_any(hidden, targets, params, moment, second, train_step):
    normalized, inv_scale = normalize(hidden[0])
    normed_bf = normalized.astype(jnp.bfloat16)
    labels = targets[0]
    shard_bf = params[0].astype(jnp.bfloat16)
    vocab_width = shard_bf.shape[1]
    weight_bf = lax.all_gather(shard_bf, "fsdp", axis=0, tiled=True)
    raw_logits = jnp.dot(normed_bf, weight_bf, preferred_element_type=jnp.float32)
    capped = jnp.tanh(raw_logits / logit_cap)
    exp_logits = jnp.exp(logit_cap * capped)
    softmax_p = exp_logits / jnp.sum(exp_logits, axis=-1, keepdims=True)
    onehot = (labels[:, None] == jnp.arange(vocab_width, dtype=jnp.int32)[None, :]).astype(
        jnp.float32
    )
    logit_grad = ((softmax_p - onehot) * (1.0 - capped * capped)).astype(jnp.bfloat16)
    full_grad = lax.dot_general(
        normed_bf, logit_grad, (((0,), (0,)), ((), ())), preferred_element_type=jnp.float32
    )
    grad_shard = lax.psum_scatter(
        full_grad.astype(jnp.bfloat16), "fsdp", scatter_dimension=0, tiled=True
    ).astype(jnp.float32)
    normed_grad = lax.dot_general(
        logit_grad, weight_bf, (((1,), (1,)), ((), ())), preferred_element_type=jnp.float32
    )
    first_mean = jnp.mean(normed_grad, axis=-1, keepdims=True)
    second_mean = jnp.mean(normed_grad * normalized, axis=-1, keepdims=True)
    grad_hidden = (inv_scale * (normed_grad - first_mean - normalized * second_mean)).astype(
        jnp.bfloat16
    )
    tcount = train_step[0].astype(jnp.float32)
    fix_one = 1.0 - jnp.exp(tcount * math.log(beta_one))
    fix_two = 1.0 - jnp.exp(tcount * math.log(beta_two))
    replica_grads = grad_shard[None]
    moment_new = beta_one * moment + (1.0 - beta_one) * replica_grads
    second_new = beta_two * second + (1.0 - beta_two) * replica_grads * replica_grads
    adam_step = moment_new / fix_one / (jnp.sqrt(second_new / fix_two) + adam_eps)
    updated = params - learn_rate * (adam_step + weight_decay * params)
    levels = lax.axis_size("replica").bit_length() - 1
    partner_values = lax.switch(
        train_step[0] % levels, [pair_with(bit_index) for bit_index in range(levels)], updated
    )
    averaged = 0.5 * (updated + partner_values)
    return (averaged, moment_new, second_new, grad_hidden[None])


near_route = [(0, 1), (1, 0), (2, 3), (3, 2)]
far_route = [(0, 2), (2, 0), (1, 3), (3, 1)]
chunk_rows = 256

f32 = jnp.float32
bf16 = jnp.bfloat16
vmem = pl.BlockSpec(memory_space=pltpu.VMEM)
smem = pl.BlockSpec(memory_space=pltpu.SMEM)
hbm = pl.BlockSpec(memory_space=pltpu.HBM)
dma = pltpu.SemaphoreType.DMA


def shaped(shape, dtype):
    return jax.ShapeDtypeStruct(shape, dtype)


def run(kernel, ins, outs, args, scratch=(), limit=10, flops=0, moved=0, out_specs=None, alias=None):
    if out_specs is None:
        out_specs = [vmem] * len(outs)
    results = pl.pallas_call(
        kernel,
        in_specs=ins,
        out_specs=out_specs,
        out_shape=outs,
        scratch_shapes=list(scratch),
        input_output_aliases=alias or {},
        compiler_params=pltpu.CompilerParams(vmem_limit_bytes=limit << 20),
        cost_estimate=pl.CostEstimate(flops=flops, bytes_accessed=moved, transcendentals=0),
    )(*args)
    return list(results)


def columns(block, width):
    return pl.ds(pl.multiple_of(block * width, 128), width)


def nt_dot(a, b):
    return lax.dot_general(a, b, (((1,), (1,)), ((), ())), preferred_element_type=f32)


def tn_dot(a, b):
    return lax.dot_general(a, b, (((0,), (0,)), ((), ())), preferred_element_type=f32)


def nn_dot(a, b):
    return jnp.dot(a, b, preferred_element_type=f32)


def fetch(src, top, held, sems):
    rows = held.shape[0]
    pieces = sems.shape[0]
    step = -(-rows // pieces // 8) * 8
    copies = []
    for piece in range(pieces):
        start = piece * step
        count = min(step, rows - start)
        copies.append(
            pltpu.make_async_copy(
                src.at[pl.ds(top + start, count), 0, :], held.at[pl.ds(start, count)], sems.at[piece]
            )
        )
        copies[-1].start()
    for copy in copies:
        copy.wait()


def round_weight_kernel(params_ref, a_ref, b_ref, whole_ref, held, sems):
    rows, total = a_ref.shape[0], held.shape[0]
    rest = total - rows
    fetch(params_ref, 0, held, sems)
    a_ref[...] = held[0:rows, :].astype(bf16)
    b_ref[0:rest, :] = held[rows:, :].astype(bf16)
    b_ref[rest:, :] = jnp.zeros((b_ref.shape[0] - rest, b_ref.shape[1]), bf16)
    whole_ref[0:rows, :] = a_ref[...]
    whole_ref[rows:, :] = b_ref[...]


def norm_kernel(count_ref, hidden_ref, normed_ref, mean_ref, inv_ref, fix_ref):
    tcount = jnp.full((1, fix_ref.shape[1]), count_ref[0].astype(f32))
    fix_ref[0:1, :] = 1.0 / (1.0 - jnp.exp(tcount * math.log(beta_one)))
    fix_ref[1:2, :] = 1.0 / (1.0 - jnp.exp(tcount * math.log(beta_two)))
    rows, width = hidden_ref.shape
    depth = normed_ref.shape[2]
    place = lax.axis_index("fsdp")
    step = 128
    for top in range(0, rows, step):
        part = pl.ds(top, step)
        values = hidden_ref[part, :].astype(f32)
        mean = jnp.mean(values, axis=-1, keepdims=True)
        center = values - mean
        inv = lax.rsqrt(jnp.mean(center * center, axis=-1, keepdims=True) + norm_eps)
        mean_ref[part, :] = mean
        inv_ref[part, :] = inv
        for slot in range(normed_ref.shape[0]):
            block = place ^ slot
            own = hidden_ref[part, columns(block, depth)].astype(f32)
            normed_ref[slot, part, :] = ((own - mean) * inv).astype(bf16)


def tiled_kernel(params_ref, moment_ref, second_ref, params_out, moment_out, second_out, sems):
    copies = []
    for slot, (src, dst) in enumerate(
        ((params_ref, params_out), (moment_ref, moment_out), (second_ref, second_out))
    ):
        copies.append(pltpu.make_async_copy(src.at[:, 0, :], dst, sems.at[slot]))
        copies[-1].start()
    for copy in copies:
        copy.wait()


def capped_exp(raw):
    capped = jnp.tanh(raw * (1.0 / logit_cap))
    return capped, jnp.exp(logit_cap * capped)


def logits_kernel(own_ref, near_ref, far_a, cross_a, far_b, normed_ref, capped_a_ref, exp_a_ref, acc_b_ref):
    rows = far_a.shape[0]
    raw = nt_dot(own_ref[0:rows, :], normed_ref[0]) + nt_dot(near_ref[0:rows, :], normed_ref[1])
    raw = raw + nt_dot(far_a[...], normed_ref[2]) + nt_dot(cross_a[...], normed_ref[3])
    capped_a_ref[...], exp_a_ref[...] = capped_exp(raw)
    acc = nt_dot(own_ref[rows:, :], normed_ref[0]) + nt_dot(near_ref[rows:, :], normed_ref[1])
    acc_b_ref[...] = acc + nt_dot(far_b[...], normed_ref[2])


def head_kernel(vocab, capped_a_ref, exp_a_ref, acc_b_ref, cross_b, normed_ref, labels_ref,
                lg_a_ref, lg_b_ref, cross_a_ref, cross_b_ref):
    rows = capped_a_ref.shape[0]
    capped_b, exp_b = capped_exp(acc_b_ref[...] + nt_dot(cross_b[...], normed_ref[3]))
    ids = lax.broadcasted_iota(jnp.int32, exp_b.shape, 0) + rows
    exp_b = jnp.where(ids < vocab, exp_b, 0.0)
    exp_a = exp_a_ref[...]
    total = jnp.sum(exp_a, axis=0, keepdims=True) + jnp.sum(exp_b, axis=0, keepdims=True)
    scale = 1.0 / total
    for top, capped, part, lg_ref, out_ref in (
        (0, capped_a_ref[...], exp_a, lg_a_ref, cross_a_ref),
        (rows, capped_b, exp_b, lg_b_ref, cross_b_ref),
    ):
        ids = lax.broadcasted_iota(jnp.int32, part.shape, 0) + top
        onehot = (ids == labels_ref[...]).astype(f32)
        logit_grad = ((part * scale - onehot) * (1.0 - capped * capped)).astype(bf16)
        lg_ref[...] = logit_grad
        out_ref[...] = nn_dot(logit_grad, normed_ref[3]).astype(bf16)


def grads_kernel(lg_a, lg_b, normed_ref, own_a, own_b, near_a, near_b, far_a, far_b):
    for slot, outs in ((2, (far_a, far_b)), (1, (near_a, near_b)), (0, (own_a, own_b))):
        for lg, out in zip((lg_a, lg_b), outs):
            out[...] = nn_dot(lg[...], normed_ref[slot]).astype(bf16)


def add_kernel(a_ref, b_ref, out_ref):
    out_ref[...] = (a_ref[...].astype(f32) + b_ref[...].astype(f32)).astype(bf16)


def hidden_grad_kernel(lg_a, lg_b, *refs):
    whole, weights_a, weights_b = refs[0:2], refs[2:4], refs[4:6]
    hidden_ref, mean_ref, inv_ref, out_ref, held = refs[6:]
    top = lg_a.shape[0]
    rows, width = hidden_ref.shape
    slots, _, depth = held.shape
    place = lax.axis_index("fsdp")
    mean, inv = mean_ref[...], inv_ref[...]
    first = jnp.zeros((rows, 1), f32)
    second = jnp.zeros((rows, 1), f32)
    for slot in range(slots):
        if slot < 2:
            block_a, block_b = whole[slot][0:top, :], whole[slot][top:, :]
        else:
            block_a, block_b = weights_a[slot - 2][...], weights_b[slot - 2][...]
        back = tn_dot(lg_a[...], block_a) + tn_dot(lg_b[...], block_b)
        held[slot] = back
        normalized = (hidden_ref[:, columns(place ^ slot, depth)].astype(f32) - mean) * inv
        first = first + jnp.sum(back, axis=-1, keepdims=True)
        second = second + jnp.sum(back * normalized, axis=-1, keepdims=True)
    first, second = first / width, second / width
    for slot in range(slots):
        part = columns(place ^ slot, depth)
        normalized = (hidden_ref[:, part].astype(f32) - mean) * inv
        out_ref[:, part] = (inv * (held[slot] - first - normalized * second)).astype(bf16)


def partial_sum_kernel(own_ref, near_ref, out_ref):
    out_ref[...] = own_ref[...].astype(f32) + near_ref[...].astype(f32)


def step_kernel(top, fix_ref, params_ref, moment_ref, second_ref, *refs):
    *terms, updated_ref, sent_ref, moment_out, second_out = refs
    rows = updated_ref.shape[0]
    part = pl.ds(top, rows)
    target = pl.ds(0, rows)
    grads = sum(ref[target, :].astype(f32) for ref in terms)
    moment_new = beta_one * moment_ref[part, :] + (1.0 - beta_one) * grads
    second_new = beta_two * second_ref[part, :] + (1.0 - beta_two) * grads * grads
    moment_out[...] = moment_new
    second_out[...] = second_new
    fix_one, fix_two = fix_ref[0:1, :], fix_ref[1:2, :]
    adam_step = moment_new * fix_one / (jnp.sqrt(second_new * fix_two) + adam_eps)
    params = params_ref[part, :]
    updated = params - learn_rate * (adam_step + weight_decay * params)
    updated_ref[...] = updated
    sent_ref[target, :] = updated.astype(bf16)
    rest = sent_ref.shape[0] - rows
    if rest:
        sent_ref[rows:, :] = jnp.zeros((rest, sent_ref.shape[1]), bf16)


def send_out(top, pairs, sems):
    copies = [
        pltpu.make_async_copy(source, target.at[pl.ds(top, source.shape[0]), 0, :], sems.at[slot])
        for slot, (source, target) in enumerate(pairs)
    ]
    for copy in copies:
        copy.start()
    return copies


def step_store_kernel(top, *refs):
    *ins, updated_ref, sent_ref, moment_out, second_out, held_moment, held_second, sems = refs
    step_kernel(top, *ins, updated_ref, sent_ref, held_moment, held_second)
    for copy in send_out(top, ((held_moment, moment_out), (held_second, second_out)), sems):
        copy.wait()


def store_kernel(top, moment_ref, second_ref, *refs):
    moment_out, second_out, sems = refs[-3:]
    for copy in send_out(top, ((moment_ref, moment_out), (second_ref, second_out)), sems):
        copy.wait()


def average_kernel(top, updated_ref, partner_ref, *refs):
    out_ref, held, sems = refs[-3:]
    rows = held.shape[0]
    held[...] = 0.5 * (updated_ref[...] + partner_ref[0:rows, :].astype(f32))
    for copy in send_out(top, ((held, out_ref),), sems):
        copy.wait()


def between_kernel(top, moment_ref, second_ref, updated_ref, partner_ref, *refs):
    moment_out, second_out, out_ref, held, sems = refs[-5:]
    copies = send_out(top, ((moment_ref, moment_out), (second_ref, second_out)), sems)
    held[...] = 0.5 * (updated_ref[...] + partner_ref[0 : held.shape[0], :].astype(f32))
    copies.append(pltpu.make_async_copy(held, out_ref.at[pl.ds(0, held.shape[0]), 0, :], sems.at[2]))
    copies[-1].start()
    for copy in copies:
        copy.wait()


def by_vocab(shard):
    return jnp.transpose(shard, (2, 0, 1))


def line_step(bit, hidden, targets, params, moment, second, train_step):
    tokens, width = hidden.shape[1:]
    depth, vocab = params.shape[1:]
    padded = -(-vocab // 16) * 16
    state_t = [by_vocab(shard) for shard in (params, moment, second)]
    heights = (chunk_rows, padded - chunk_rows)
    tops = (0, chunk_rows)
    counts = (chunk_rows, vocab - chunk_rows)
    shards = [shaped((height, depth), bf16) for height in heights]
    held = [pltpu.VMEM((count, depth), f32) for count in counts]
    state = shaped((vocab, depth), f32)
    state_out = pltpu.HBM((vocab, 1, depth), f32)
    dot_flops = 2 * padded * tokens * depth

    def hop(block, route):
        return lax.ppermute(block, "fsdp", route)

    whole_shard = shaped((padded, depth), bf16)
    *own, own_whole = run(
        round_weight_kernel,
        [hbm],
        [*shards, whole_shard],
        (state_t[0],),
        [pltpu.VMEM((vocab, depth), f32), dma((4,))],
    )
    far = [hop(block, far_route) for block in own]
    near = hop(own_whole, near_route)
    normed, mean, inv, fix = run(
        norm_kernel,
        [smem, vmem],
        [shaped((4, tokens, depth), bf16), shaped((tokens, 1), f32), shaped((tokens, 1), f32), shaped((2, depth), f32)],
        (train_step, hidden[0]),
        flops=10 * tokens * width,
        moved=4 * tokens * width,
    )
    tiled = run(tiled_kernel, [hbm] * 3, [state] * 3, state_t, [dma((3,))])
    far[0], normed, *tiled = lax.optimization_barrier((far[0], normed, *tiled))
    cross = [hop(block, near_route) for block in far]
    capped_a, exp_a, acc_b = run(
        logits_kernel,
        [vmem] * 6,
        [shaped((height, tokens), f32) for height in (heights[0], *heights)],
        (own_whole, near, far[0], cross[0], far[1], normed),
        flops=3 * dot_flops,
    )
    lg_a, lg_b, cross_part_a, cross_part_b = run(
        lambda *refs: head_kernel(vocab, *refs),
        [vmem] * 6,
        [shaped((height, tokens), bf16) for height in heights] + shards,
        (capped_a, exp_a, acc_b, cross[1], normed, targets),
        flops=2 * dot_flops,
    )
    got_a, got_b = [hop(block, near_route) for block in (cross_part_a, cross_part_b)]
    own_a, own_b, near_a, near_b, far_a, far_b = run(
        grads_kernel, [vmem] * 3, shards * 3, (lg_a, lg_b, normed), flops=3 * dot_flops
    )
    sum_a = run(add_kernel, [vmem] * 2, [shards[0]], (far_a, got_a))[0]
    near_a, later_a = lax.optimization_barrier((near_a, sum_a))
    got_far_a, got_near_a = hop(sum_a, far_route), hop(near_a, near_route)
    got_b, later_a = lax.optimization_barrier((got_b, later_a))
    sum_b = run(add_kernel, [vmem] * 2, [shards[1]], (far_b, got_b))[0]
    lg_late, sum_b = lax.optimization_barrier((lg_a, sum_b))
    grad_hidden = run(
        hidden_grad_kernel,
        [vmem] * 11,
        [shaped((tokens, width), bf16)],
        (lg_late, lg_b, own_whole, near, far[0], cross[0], far[1], cross[1], hidden[0], mean, inv),
        [pltpu.VMEM((4, tokens, depth), f32)],
        flops=4 * dot_flops,
    )[0]
    state_part = [shaped((count, depth), f32) for count in counts]
    if bit:
        sums = [shaped(shard.shape, f32) for shard in shards]
        local_a = run(partial_sum_kernel, [vmem] * 2, sums[:1], (own_a, got_near_a))[0]
        got_far_a, local_a, sum_b, near_b, grad_hidden = lax.optimization_barrier(
            (got_far_a, local_a, sum_b, near_b, grad_hidden)
        )
        got_near_b, got_far_b = hop(near_b, near_route), hop(sum_b, far_route)
        local_b = run(partial_sum_kernel, [vmem] * 2, sums[1:], (own_b, got_near_b))[0]
        terms = ((local_a, got_far_a), (local_b, got_far_b))
    else:
        got_far_a, grad_hidden = lax.optimization_barrier((got_far_a, grad_hidden))
        got_far_b, got_near_b = hop(sum_b, far_route), hop(near_b, near_route)
        terms = ((own_a, got_near_a, got_far_a), (own_b, got_near_b, got_far_b))
    moments, averaged = [], []

    def step(index, kernel, state_new, scratch=()):
        updated, sent, *state_new = run(
            functools.partial(kernel, tops[index]),
            [vmem] * (4 + len(terms[index])),
            [state_part[index], shards[index], *state_new],
            (fix, *tiled, *terms[index]),
            scratch,
            out_specs=[vmem, vmem] + [hbm if scratch else vmem] * 2,
        )
        return updated, from_partner(sent, "replica", bit), state_new

    def store(index, state_new, moments):
        return run(
            functools.partial(store_kernel, tops[index]),
            [vmem] * 2 + [hbm] * len(moments),
            [state_out] * 2,
            (*state_new, *moments),
            [dma((2,))],
            out_specs=[hbm] * 2,
            alias={2: 0, 3: 1} if moments else None,
        )

    def average(index, updated, partner, averaged):
        return run(
            functools.partial(average_kernel, tops[index]),
            [vmem] * 2 + [hbm] * len(averaged),
            [state_out],
            (updated, partner, *averaged),
            [held[index], dma((1,))],
            out_specs=[hbm],
            alias={2: 0} if averaged else None,
        )

    if bit:
        updated_a, partner_a, state_a = step(0, step_kernel, state_part[:1] * 2)
    else:
        scratch = [held[0], held[0], dma((2,))]
        updated_a, partner_a, moments = step(0, step_store_kernel, [state_out] * 2, scratch)
    updated_b, partner_b, state_b = step(1, step_kernel, state_part[1:] * 2)
    partner_a, updated_b = lax.optimization_barrier((partner_a, updated_b))
    if bit:
        averaged = average(0, updated_a, partner_a, averaged)
        moments = store(0, state_a, moments)
        moments = store(1, state_b, moments)
    else:
        *moments, averaged = run(
            functools.partial(between_kernel, tops[1]),
            [vmem] * 4 + [hbm] * 2,
            [state_out] * 3,
            (*state_b, updated_a, partner_a, *moments),
            [held[0], dma((3,))],
            out_specs=[hbm] * 3,
            alias={4: 0, 5: 1},
        )
        averaged = [averaged]
    averaged = average(1, updated_b, partner_b, averaged)
    outs = [jnp.transpose(out, (1, 2, 0)) for out in (averaged[0], *moments)]
    return (*outs, grad_hidden[None])


def local_line(hidden, targets, params, moment, second, train_step):
    levels = lax.axis_size("replica").bit_length() - 1
    branches = [functools.partial(line_step, bit) for bit in range(levels)]
    level = lax.rem(train_step[0], levels)
    return lax.switch(level, branches, hidden, targets, params, moment, second, train_step)


def local(hidden, targets, params, moment, second, train_step):
    four = lax.axis_size("fsdp") == 4 and params.shape[1] % 128 == 0 and hidden.shape[1] % 128 == 0
    four = four and params.shape[2] > chunk_rows
    chosen = local_line if four else local_any
    return chosen(hidden, targets, params, moment, second, train_step)


def solution(mesh):
    placed = (
        P("replica", ("groups", "fsdp"), None),
        P("replica", ("groups", "fsdp")),
        P("replica", ("groups", "fsdp"), None),
        P("replica", ("groups", "fsdp"), None),
        P("replica", ("groups", "fsdp"), None),
        P(),
    )
    return jax.shard_map(
        local,
        mesh=mesh,
        in_specs=placed,
        out_specs=(
            P("replica", ("groups", "fsdp"), None),
            P("replica", ("groups", "fsdp"), None),
            P("replica", ("groups", "fsdp"), None),
            P("replica", ("groups", "fsdp"), None),
        ),
        check_vma=False,
    )
```

```python
import functools
import math

import jax
import jax.numpy as jnp
from jax import lax
from jax.experimental import pallas as pl
from jax.experimental.pallas import tpu as pltpu
from jax.sharding import PartitionSpec as P

norm_eps = 1e-05
logit_cap = 30.0
learn_rate = 0.001
weight_decay = 0.1
beta_one = 0.9
beta_two = 0.999
adam_eps = 1e-08


def shortened(x):
    return jax.tree.map(lambda a: a.astype(jnp.bfloat16) if a.dtype == jnp.float32 else a, x)


def from_partner(block, axis, stride):
    count = lax.axis_size(axis)
    route = []
    for low in range(count):
        high = low | 1 << stride
        if high != low and high < count:
            route += [(low, high), (high, low)]
    return lax.ppermute(block, axis, route)


def normalize(token_block):
    values = token_block.astype(jnp.float32)
    center = values - jnp.mean(values, axis=-1, keepdims=True)
    inv_scale = lax.rsqrt(jnp.mean(center * center, axis=-1, keepdims=True) + norm_eps)
    return (center * inv_scale, inv_scale)


def pair_with(bit_index):

    def swap_values(values):
        return jax.tree.map(
            lambda part, own: part.astype(own.dtype),
            from_partner(shortened(values), "replica", bit_index),
            values,
        )

    return swap_values


def local_any(hidden, targets, params, moment, second, train_step):
    normalized, inv_scale = normalize(hidden[0])
    normed_bf = normalized.astype(jnp.bfloat16)
    labels = targets[0]
    shard_bf = params[0].astype(jnp.bfloat16)
    vocab_width = shard_bf.shape[1]
    weight_bf = lax.all_gather(shard_bf, "fsdp", axis=0, tiled=True)
    raw_logits = jnp.dot(normed_bf, weight_bf, preferred_element_type=jnp.float32)
    capped = jnp.tanh(raw_logits / logit_cap)
    exp_logits = jnp.exp(logit_cap * capped)
    softmax_p = exp_logits / jnp.sum(exp_logits, axis=-1, keepdims=True)
    onehot = (labels[:, None] == jnp.arange(vocab_width, dtype=jnp.int32)[None, :]).astype(
        jnp.float32
    )
    logit_grad = ((softmax_p - onehot) * (1.0 - capped * capped)).astype(jnp.bfloat16)
    full_grad = lax.dot_general(
        normed_bf, logit_grad, (((0,), (0,)), ((), ())), preferred_element_type=jnp.float32
    )
    grad_shard = lax.psum_scatter(
        full_grad.astype(jnp.bfloat16), "fsdp", scatter_dimension=0, tiled=True
    ).astype(jnp.float32)
    normed_grad = lax.dot_general(
        logit_grad, weight_bf, (((1,), (1,)), ((), ())), preferred_element_type=jnp.float32
    )
    first_mean = jnp.mean(normed_grad, axis=-1, keepdims=True)
    second_mean = jnp.mean(normed_grad * normalized, axis=-1, keepdims=True)
    grad_hidden = (inv_scale * (normed_grad - first_mean - normalized * second_mean)).astype(
        jnp.bfloat16
    )
    tcount = train_step[0].astype(jnp.float32)
    fix_one = 1.0 - jnp.exp(tcount * math.log(beta_one))
    fix_two = 1.0 - jnp.exp(tcount * math.log(beta_two))
    replica_grads = grad_shard[None]
    moment_new = beta_one * moment + (1.0 - beta_one) * replica_grads
    second_new = beta_two * second + (1.0 - beta_two) * replica_grads * replica_grads
    adam_step = moment_new / fix_one / (jnp.sqrt(second_new / fix_two) + adam_eps)
    updated = params - learn_rate * (adam_step + weight_decay * params)
    levels = lax.axis_size("replica").bit_length() - 1
    partner_values = lax.switch(
        train_step[0] % levels, [pair_with(bit_index) for bit_index in range(levels)], updated
    )
    averaged = 0.5 * (updated + partner_values)
    return (averaged, moment_new, second_new, grad_hidden[None])


near_route = [(0, 1), (1, 0), (2, 3), (3, 2)]
far_route = [(0, 2), (2, 0), (1, 3), (3, 1)]
chunk_rows = 256

f32 = jnp.float32
bf16 = jnp.bfloat16
vmem = pl.BlockSpec(memory_space=pltpu.VMEM)
smem = pl.BlockSpec(memory_space=pltpu.SMEM)
hbm = pl.BlockSpec(memory_space=pltpu.HBM)
dma = pltpu.SemaphoreType.DMA


def shaped(shape, dtype):
    return jax.ShapeDtypeStruct(shape, dtype)


def run(kernel, ins, outs, args, scratch=(), limit=10, flops=0, moved=0, out_specs=None, alias=None):
    if out_specs is None:
        out_specs = [vmem] * len(outs)
    results = pl.pallas_call(
        kernel,
        in_specs=ins,
        out_specs=out_specs,
        out_shape=outs,
        scratch_shapes=list(scratch),
        input_output_aliases=alias or {},
        compiler_params=pltpu.CompilerParams(vmem_limit_bytes=limit << 20),
        cost_estimate=pl.CostEstimate(flops=flops, bytes_accessed=moved, transcendentals=0),
    )(*args)
    return list(results)


def columns(block, width):
    return pl.ds(pl.multiple_of(block * width, 128), width)


def nt_dot(a, b):
    return lax.dot_general(a, b, (((1,), (1,)), ((), ())), preferred_element_type=f32)


def tn_dot(a, b):
    return lax.dot_general(a, b, (((0,), (0,)), ((), ())), preferred_element_type=f32)


def nn_dot(a, b):
    return jnp.dot(a, b, preferred_element_type=f32)


def fetch(src, top, held, sems):
    rows = held.shape[0]
    pieces = sems.shape[0]
    step = -(-rows // pieces // 8) * 8
    copies = []
    for piece in range(pieces):
        start = piece * step
        count = min(step, rows - start)
        copies.append(
            pltpu.make_async_copy(
                src.at[pl.ds(top + start, count), 0, :], held.at[pl.ds(start, count)], sems.at[piece]
            )
        )
        copies[-1].start()
    for copy in copies:
        copy.wait()


def round_weight_kernel(params_ref, a_ref, b_ref, whole_ref, held, sems):
    rows, total = a_ref.shape[0], held.shape[0]
    rest = total - rows
    fetch(params_ref, 0, held, sems)
    a_ref[...] = held[0:rows, :].astype(bf16)
    b_ref[0:rest, :] = held[rows:, :].astype(bf16)
    b_ref[rest:, :] = jnp.zeros((b_ref.shape[0] - rest, b_ref.shape[1]), bf16)
    whole_ref[0:rows, :] = a_ref[...]
    whole_ref[rows:, :] = b_ref[...]


def norm_kernel(count_ref, hidden_ref, normed_ref, mean_ref, inv_ref, fix_ref):
    tcount = jnp.full((1, fix_ref.shape[1]), count_ref[0].astype(f32))
    fix_ref[0:1, :] = 1.0 / (1.0 - jnp.exp(tcount * math.log(beta_one)))
    fix_ref[1:2, :] = 1.0 / (1.0 - jnp.exp(tcount * math.log(beta_two)))
    rows, width = hidden_ref.shape
    depth = normed_ref.shape[2]
    place = lax.axis_index("fsdp")
    step = 128
    for top in range(0, rows, step):
        part = pl.ds(top, step)
        values = hidden_ref[part, :].astype(f32)
        mean = jnp.mean(values, axis=-1, keepdims=True)
        center = values - mean
        inv = lax.rsqrt(jnp.mean(center * center, axis=-1, keepdims=True) + norm_eps)
        mean_ref[part, :] = mean
        inv_ref[part, :] = inv
        for slot in range(normed_ref.shape[0]):
            block = place ^ slot
            own = hidden_ref[part, columns(block, depth)].astype(f32)
            normed_ref[slot, part, :] = ((own - mean) * inv).astype(bf16)


def tiled_kernel(params_ref, moment_ref, second_ref, params_out, moment_out, second_out, sems):
    copies = []
    for slot, (src, dst) in enumerate(
        ((params_ref, params_out), (moment_ref, moment_out), (second_ref, second_out))
    ):
        copies.append(pltpu.make_async_copy(src.at[:, 0, :], dst, sems.at[slot]))
        copies[-1].start()
    for copy in copies:
        copy.wait()


def capped_exp(raw):
    capped = jnp.tanh(raw * (1.0 / logit_cap))
    return capped, jnp.exp(logit_cap * capped)


def logits_kernel(own_ref, near_ref, far_a, cross_a, far_b, normed_ref, capped_a_ref, exp_a_ref, acc_b_ref):
    rows = far_a.shape[0]
    raw = nt_dot(own_ref[0:rows, :], normed_ref[0]) + nt_dot(near_ref[0:rows, :], normed_ref[1])
    raw = raw + nt_dot(far_a[...], normed_ref[2]) + nt_dot(cross_a[...], normed_ref[3])
    capped_a_ref[...], exp_a_ref[...] = capped_exp(raw)
    acc = nt_dot(own_ref[rows:, :], normed_ref[0]) + nt_dot(near_ref[rows:, :], normed_ref[1])
    acc_b_ref[...] = acc + nt_dot(far_b[...], normed_ref[2])


def head_kernel(vocab, capped_a_ref, exp_a_ref, acc_b_ref, cross_b, normed_ref, labels_ref,
                lg_a_ref, lg_b_ref, cross_a_ref, cross_b_ref):
    rows = capped_a_ref.shape[0]
    capped_b, exp_b = capped_exp(acc_b_ref[...] + nt_dot(cross_b[...], normed_ref[3]))
    ids = lax.broadcasted_iota(jnp.int32, exp_b.shape, 0) + rows
    exp_b = jnp.where(ids < vocab, exp_b, 0.0)
    exp_a = exp_a_ref[...]
    total = jnp.sum(exp_a, axis=0, keepdims=True) + jnp.sum(exp_b, axis=0, keepdims=True)
    scale = 1.0 / total
    for top, capped, part, lg_ref, out_ref in (
        (0, capped_a_ref[...], exp_a, lg_a_ref, cross_a_ref),
        (rows, capped_b, exp_b, lg_b_ref, cross_b_ref),
    ):
        ids = lax.broadcasted_iota(jnp.int32, part.shape, 0) + top
        onehot = (ids == labels_ref[...]).astype(f32)
        logit_grad = ((part * scale - onehot) * (1.0 - capped * capped)).astype(bf16)
        lg_ref[...] = logit_grad
        out_ref[...] = nn_dot(logit_grad, normed_ref[3]).astype(bf16)


def grads_kernel(lg_a, lg_b, normed_ref, own_a, own_b, near_a, near_b, far_a, far_b):
    for slot, outs in ((2, (far_a, far_b)), (1, (near_a, near_b)), (0, (own_a, own_b))):
        for lg, out in zip((lg_a, lg_b), outs):
            out[...] = nn_dot(lg[...], normed_ref[slot]).astype(bf16)


def add_kernel(a_ref, b_ref, out_ref):
    out_ref[...] = (a_ref[...].astype(f32) + b_ref[...].astype(f32)).astype(bf16)


def hidden_grad_kernel(lg_a, lg_b, *refs):
    whole, weights_a, weights_b = refs[0:2], refs[2:4], refs[4:6]
    hidden_ref, mean_ref, inv_ref, out_ref, held = refs[6:]
    top = lg_a.shape[0]
    rows, width = hidden_ref.shape
    slots, _, depth = held.shape
    place = lax.axis_index("fsdp")
    mean, inv = mean_ref[...], inv_ref[...]
    first = jnp.zeros((rows, 1), f32)
    second = jnp.zeros((rows, 1), f32)
    for slot in range(slots):
        if slot < 2:
            block_a, block_b = whole[slot][0:top, :], whole[slot][top:, :]
        else:
            block_a, block_b = weights_a[slot - 2][...], weights_b[slot - 2][...]
        back = tn_dot(lg_a[...], block_a) + tn_dot(lg_b[...], block_b)
        held[slot] = back
        normalized = (hidden_ref[:, columns(place ^ slot, depth)].astype(f32) - mean) * inv
        first = first + jnp.sum(back, axis=-1, keepdims=True)
        second = second + jnp.sum(back * normalized, axis=-1, keepdims=True)
    first, second = first / width, second / width
    for slot in range(slots):
        part = columns(place ^ slot, depth)
        normalized = (hidden_ref[:, part].astype(f32) - mean) * inv
        out_ref[:, part] = (inv * (held[slot] - first - normalized * second)).astype(bf16)


def partial_sum_kernel(own_ref, near_ref, out_ref):
    out_ref[...] = own_ref[...].astype(f32) + near_ref[...].astype(f32)


def step_kernel(top, fix_ref, params_ref, moment_ref, second_ref, *refs):
    *terms, updated_ref, sent_ref, moment_out, second_out = refs
    rows = updated_ref.shape[0]
    part = pl.ds(top, rows)
    target = pl.ds(0, rows)
    grads = sum(ref[target, :].astype(f32) for ref in terms)
    moment_new = beta_one * moment_ref[part, :] + (1.0 - beta_one) * grads
    second_new = beta_two * second_ref[part, :] + (1.0 - beta_two) * grads * grads
    moment_out[...] = moment_new
    second_out[...] = second_new
    fix_one, fix_two = fix_ref[0:1, :], fix_ref[1:2, :]
    adam_step = moment_new * fix_one / (jnp.sqrt(second_new * fix_two) + adam_eps)
    params = params_ref[part, :]
    updated = params - learn_rate * (adam_step + weight_decay * params)
    updated_ref[...] = updated
    sent_ref[target, :] = updated.astype(bf16)
    rest = sent_ref.shape[0] - rows
    if rest:
        sent_ref[rows:, :] = jnp.zeros((rest, sent_ref.shape[1]), bf16)


def send_out(top, pairs, sems):
    copies = [
        pltpu.make_async_copy(source, target.at[pl.ds(top, source.shape[0]), 0, :], sems.at[slot])
        for slot, (source, target) in enumerate(pairs)
    ]
    for copy in copies:
        copy.start()
    return copies


def step_store_kernel(top, *refs):
    *ins, updated_ref, sent_ref, moment_out, second_out, held_moment, held_second, sems = refs
    step_kernel(top, *ins, updated_ref, sent_ref, held_moment, held_second)
    for copy in send_out(top, ((held_moment, moment_out), (held_second, second_out)), sems):
        copy.wait()


def store_kernel(top, moment_ref, second_ref, *refs):
    moment_out, second_out, sems = refs[-3:]
    for copy in send_out(top, ((moment_ref, moment_out), (second_ref, second_out)), sems):
        copy.wait()


def average_kernel(top, updated_ref, partner_ref, *refs):
    out_ref, held, sems = refs[-3:]
    rows = held.shape[0]
    step = -(-rows // sems.shape[0] // 16) * 16
    copies = []
    for piece, start in enumerate(range(0, rows, step)):
        count = min(step, rows - start)
        part = pl.ds(start, count)
        held[part, :] = 0.5 * (updated_ref[part, :] + partner_ref[part, :].astype(f32))
        copies.append(
            pltpu.make_async_copy(held.at[part], out_ref.at[pl.ds(top + start, count), 0, :], sems.at[piece])
        )
        copies[-1].start()
    for copy in copies:
        copy.wait()


def between_kernel(top, moment_ref, second_ref, updated_ref, partner_ref, *refs):
    moment_out, second_out, out_ref, held, sems = refs[-5:]
    copies = send_out(top, ((moment_ref, moment_out), (second_ref, second_out)), sems)
    held[...] = 0.5 * (updated_ref[...] + partner_ref[0 : held.shape[0], :].astype(f32))
    copies.append(pltpu.make_async_copy(held, out_ref.at[pl.ds(0, held.shape[0]), 0, :], sems.at[2]))
    copies[-1].start()
    for copy in copies:
        copy.wait()


def by_vocab(shard):
    return jnp.transpose(shard, (2, 0, 1))


def line_step(bit, hidden, targets, params, moment, second, train_step):
    tokens, width = hidden.shape[1:]
    depth, vocab = params.shape[1:]
    padded = -(-vocab // 16) * 16
    state_t = [by_vocab(shard) for shard in (params, moment, second)]
    heights = (chunk_rows, padded - chunk_rows)
    tops = (0, chunk_rows)
    counts = (chunk_rows, vocab - chunk_rows)
    shards = [shaped((height, depth), bf16) for height in heights]
    held = [pltpu.VMEM((count, depth), f32) for count in counts]
    state = shaped((vocab, depth), f32)
    state_out = pltpu.HBM((vocab, 1, depth), f32)
    dot_flops = 2 * padded * tokens * depth

    def hop(block, route):
        return lax.ppermute(block, "fsdp", route)

    whole_shard = shaped((padded, depth), bf16)
    *own, own_whole = run(
        round_weight_kernel,
        [hbm],
        [*shards, whole_shard],
        (state_t[0],),
        [pltpu.VMEM((vocab, depth), f32), dma((4,))],
    )
    far = [hop(block, far_route) for block in own]
    near = hop(own_whole, near_route)
    normed, mean, inv, fix = run(
        norm_kernel,
        [smem, vmem],
        [shaped((4, tokens, depth), bf16), shaped((tokens, 1), f32), shaped((tokens, 1), f32), shaped((2, depth), f32)],
        (train_step, hidden[0]),
        flops=10 * tokens * width,
        moved=4 * tokens * width,
    )
    tiled = run(tiled_kernel, [hbm] * 3, [state] * 3, state_t, [dma((3,))])
    far[0], normed, *tiled = lax.optimization_barrier((far[0], normed, *tiled))
    cross = [hop(block, near_route) for block in far]
    capped_a, exp_a, acc_b = run(
        logits_kernel,
        [vmem] * 6,
        [shaped((height, tokens), f32) for height in (heights[0], *heights)],
        (own_whole, near, far[0], cross[0], far[1], normed),
        flops=3 * dot_flops,
    )
    lg_a, lg_b, cross_part_a, cross_part_b = run(
        lambda *refs: head_kernel(vocab, *refs),
        [vmem] * 6,
        [shaped((height, tokens), bf16) for height in heights] + shards,
        (capped_a, exp_a, acc_b, cross[1], normed, targets),
        flops=2 * dot_flops,
    )
    got_a, got_b = [hop(block, near_route) for block in (cross_part_a, cross_part_b)]
    own_a, own_b, near_a, near_b, far_a, far_b = run(
        grads_kernel, [vmem] * 3, shards * 3, (lg_a, lg_b, normed), flops=3 * dot_flops
    )
    sum_a = run(add_kernel, [vmem] * 2, [shards[0]], (far_a, got_a))[0]
    near_a, later_a = lax.optimization_barrier((near_a, sum_a))
    got_far_a, got_near_a = hop(sum_a, far_route), hop(near_a, near_route)
    got_b, later_a = lax.optimization_barrier((got_b, later_a))
    sum_b = run(add_kernel, [vmem] * 2, [shards[1]], (far_b, got_b))[0]
    lg_late, sum_b = lax.optimization_barrier((lg_a, sum_b))
    grad_hidden = run(
        hidden_grad_kernel,
        [vmem] * 11,
        [shaped((tokens, width), bf16)],
        (lg_late, lg_b, own_whole, near, far[0], cross[0], far[1], cross[1], hidden[0], mean, inv),
        [pltpu.VMEM((4, tokens, depth), f32)],
        flops=4 * dot_flops,
    )[0]
    state_part = [shaped((count, depth), f32) for count in counts]
    if bit:
        sums = [shaped(shard.shape, f32) for shard in shards]
        local_a = run(partial_sum_kernel, [vmem] * 2, sums[:1], (own_a, got_near_a))[0]
        got_far_a, local_a, sum_b, near_b, grad_hidden = lax.optimization_barrier(
            (got_far_a, local_a, sum_b, near_b, grad_hidden)
        )
        got_near_b, got_far_b = hop(near_b, near_route), hop(sum_b, far_route)
        local_b = run(partial_sum_kernel, [vmem] * 2, sums[1:], (own_b, got_near_b))[0]
        terms = ((local_a, got_far_a), (local_b, got_far_b))
    else:
        got_far_a, grad_hidden = lax.optimization_barrier((got_far_a, grad_hidden))
        got_far_b, got_near_b = hop(sum_b, far_route), hop(near_b, near_route)
        terms = ((own_a, got_near_a, got_far_a), (own_b, got_near_b, got_far_b))
    moments, averaged = [], []

    def step(index, kernel, state_new, scratch=()):
        updated, sent, *state_new = run(
            functools.partial(kernel, tops[index]),
            [vmem] * (4 + len(terms[index])),
            [state_part[index], shards[index], *state_new],
            (fix, *tiled, *terms[index]),
            scratch,
            out_specs=[vmem, vmem] + [hbm if scratch else vmem] * 2,
        )
        return updated, from_partner(sent, "replica", bit), state_new

    def store(index, state_new, moments):
        return run(
            functools.partial(store_kernel, tops[index]),
            [vmem] * 2 + [hbm] * len(moments),
            [state_out] * 2,
            (*state_new, *moments),
            [dma((2,))],
            out_specs=[hbm] * 2,
            alias={2: 0, 3: 1} if moments else None,
        )

    def average(index, updated, partner, averaged):
        return run(
            functools.partial(average_kernel, tops[index]),
            [vmem] * 2 + [hbm] * len(averaged),
            [state_out],
            (updated, partner, *averaged),
            [held[index], dma((4,))],
            out_specs=[hbm],
            alias={2: 0} if averaged else None,
        )

    if bit:
        updated_a, partner_a, state_a = step(0, step_kernel, state_part[:1] * 2)
    else:
        scratch = [held[0], held[0], dma((2,))]
        updated_a, partner_a, moments = step(0, step_store_kernel, [state_out] * 2, scratch)
    updated_b, partner_b, state_b = step(1, step_kernel, state_part[1:] * 2)
    partner_a, updated_b = lax.optimization_barrier((partner_a, updated_b))
    if bit:
        averaged = average(0, updated_a, partner_a, averaged)
        moments = store(0, state_a, moments)
        moments = store(1, state_b, moments)
    else:
        *moments, averaged = run(
            functools.partial(between_kernel, tops[1]),
            [vmem] * 4 + [hbm] * 2,
            [state_out] * 3,
            (*state_b, updated_a, partner_a, *moments),
            [held[0], dma((3,))],
            out_specs=[hbm] * 3,
            alias={4: 0, 5: 1},
        )
        averaged = [averaged]
    averaged = average(1, updated_b, partner_b, averaged)
    outs = [jnp.transpose(out, (1, 2, 0)) for out in (averaged[0], *moments)]
    return (*outs, grad_hidden[None])


def local_line(hidden, targets, params, moment, second, train_step):
    levels = lax.axis_size("replica").bit_length() - 1
    branches = [functools.partial(line_step, bit) for bit in range(levels)]
    level = lax.rem(train_step[0], levels)
    return lax.switch(level, branches, hidden, targets, params, moment, second, train_step)


def local(hidden, targets, params, moment, second, train_step):
    four = lax.axis_size("fsdp") == 4 and params.shape[1] % 128 == 0 and hidden.shape[1] % 128 == 0
    four = four and params.shape[2] > chunk_rows
    chosen = local_line if four else local_any
    return chosen(hidden, targets, params, moment, second, train_step)


def solution(mesh):
    placed = (
        P("replica", ("groups", "fsdp"), None),
        P("replica", ("groups", "fsdp")),
        P("replica", ("groups", "fsdp"), None),
        P("replica", ("groups", "fsdp"), None),
        P("replica", ("groups", "fsdp"), None),
        P(),
    )
    return jax.shard_map(
        local,
        mesh=mesh,
        in_specs=placed,
        out_specs=(
            P("replica", ("groups", "fsdp"), None),
            P("replica", ("groups", "fsdp"), None),
            P("replica", ("groups", "fsdp"), None),
            P("replica", ("groups", "fsdp"), None),
        ),
        check_vma=False,
    )
```

```python
import functools
import math

import jax
import jax.numpy as jnp
from jax import lax
from jax.experimental import pallas as pl
from jax.experimental.pallas import tpu as pltpu
from jax.sharding import PartitionSpec as P

norm_eps = 1e-05
logit_cap = 30.0
learn_rate = 0.001
weight_decay = 0.1
beta_one = 0.9
beta_two = 0.999
adam_eps = 1e-08


def shortened(x):
    return jax.tree.map(lambda a: a.astype(jnp.bfloat16) if a.dtype == jnp.float32 else a, x)


def from_partner(block, axis, stride):
    count = lax.axis_size(axis)
    route = []
    for low in range(count):
        high = low | 1 << stride
        if high != low and high < count:
            route += [(low, high), (high, low)]
    return lax.ppermute(block, axis, route)


def normalize(token_block):
    values = token_block.astype(jnp.float32)
    center = values - jnp.mean(values, axis=-1, keepdims=True)
    inv_scale = lax.rsqrt(jnp.mean(center * center, axis=-1, keepdims=True) + norm_eps)
    return (center * inv_scale, inv_scale)


def pair_with(bit_index):

    def swap_values(values):
        return jax.tree.map(
            lambda part, own: part.astype(own.dtype),
            from_partner(shortened(values), "replica", bit_index),
            values,
        )

    return swap_values


def local_any(hidden, targets, params, moment, second, train_step):
    normalized, inv_scale = normalize(hidden[0])
    normed_bf = normalized.astype(jnp.bfloat16)
    labels = targets[0]
    shard_bf = params[0].astype(jnp.bfloat16)
    vocab_width = shard_bf.shape[1]
    weight_bf = lax.all_gather(shard_bf, "fsdp", axis=0, tiled=True)
    raw_logits = jnp.dot(normed_bf, weight_bf, preferred_element_type=jnp.float32)
    capped = jnp.tanh(raw_logits / logit_cap)
    exp_logits = jnp.exp(logit_cap * capped)
    softmax_p = exp_logits / jnp.sum(exp_logits, axis=-1, keepdims=True)
    onehot = (labels[:, None] == jnp.arange(vocab_width, dtype=jnp.int32)[None, :]).astype(
        jnp.float32
    )
    logit_grad = ((softmax_p - onehot) * (1.0 - capped * capped)).astype(jnp.bfloat16)
    full_grad = lax.dot_general(
        normed_bf, logit_grad, (((0,), (0,)), ((), ())), preferred_element_type=jnp.float32
    )
    grad_shard = lax.psum_scatter(
        full_grad.astype(jnp.bfloat16), "fsdp", scatter_dimension=0, tiled=True
    ).astype(jnp.float32)
    normed_grad = lax.dot_general(
        logit_grad, weight_bf, (((1,), (1,)), ((), ())), preferred_element_type=jnp.float32
    )
    first_mean = jnp.mean(normed_grad, axis=-1, keepdims=True)
    second_mean = jnp.mean(normed_grad * normalized, axis=-1, keepdims=True)
    grad_hidden = (inv_scale * (normed_grad - first_mean - normalized * second_mean)).astype(
        jnp.bfloat16
    )
    tcount = train_step[0].astype(jnp.float32)
    fix_one = 1.0 - jnp.exp(tcount * math.log(beta_one))
    fix_two = 1.0 - jnp.exp(tcount * math.log(beta_two))
    replica_grads = grad_shard[None]
    moment_new = beta_one * moment + (1.0 - beta_one) * replica_grads
    second_new = beta_two * second + (1.0 - beta_two) * replica_grads * replica_grads
    adam_step = moment_new / fix_one / (jnp.sqrt(second_new / fix_two) + adam_eps)
    updated = params - learn_rate * (adam_step + weight_decay * params)
    levels = lax.axis_size("replica").bit_length() - 1
    partner_values = lax.switch(
        train_step[0] % levels, [pair_with(bit_index) for bit_index in range(levels)], updated
    )
    averaged = 0.5 * (updated + partner_values)
    return (averaged, moment_new, second_new, grad_hidden[None])


near_route = [(0, 1), (1, 0), (2, 3), (3, 2)]
far_route = [(0, 2), (2, 0), (1, 3), (3, 1)]
chunk_rows = 256

f32 = jnp.float32
bf16 = jnp.bfloat16
vmem = pl.BlockSpec(memory_space=pltpu.VMEM)
smem = pl.BlockSpec(memory_space=pltpu.SMEM)
hbm = pl.BlockSpec(memory_space=pltpu.HBM)
dma = pltpu.SemaphoreType.DMA


def shaped(shape, dtype):
    return jax.ShapeDtypeStruct(shape, dtype)


def run(kernel, ins, outs, args, scratch=(), limit=10, flops=0, moved=0, out_specs=None, alias=None):
    if out_specs is None:
        out_specs = [vmem] * len(outs)
    results = pl.pallas_call(
        kernel,
        in_specs=ins,
        out_specs=out_specs,
        out_shape=outs,
        scratch_shapes=list(scratch),
        input_output_aliases=alias or {},
        compiler_params=pltpu.CompilerParams(vmem_limit_bytes=limit << 20),
        cost_estimate=pl.CostEstimate(flops=flops, bytes_accessed=moved, transcendentals=0),
    )(*args)
    return list(results)


def columns(block, width):
    return pl.ds(pl.multiple_of(block * width, 128), width)


def nt_dot(a, b):
    return lax.dot_general(a, b, (((1,), (1,)), ((), ())), preferred_element_type=f32)


def tn_dot(a, b):
    return lax.dot_general(a, b, (((0,), (0,)), ((), ())), preferred_element_type=f32)


def nn_dot(a, b):
    return jnp.dot(a, b, preferred_element_type=f32)


def fetch(src, top, held, sems):
    rows = held.shape[0]
    pieces = sems.shape[0]
    step = -(-rows // pieces // 8) * 8
    copies = []
    for piece in range(pieces):
        start = piece * step
        count = min(step, rows - start)
        copies.append(
            pltpu.make_async_copy(
                src.at[pl.ds(top + start, count), 0, :], held.at[pl.ds(start, count)], sems.at[piece]
            )
        )
        copies[-1].start()
    for copy in copies:
        copy.wait()


def round_weight_kernel(params_ref, a_ref, b_ref, whole_ref, held, sems):
    rows, total = a_ref.shape[0], held.shape[0]
    rest = total - rows
    fetch(params_ref, 0, held, sems)
    a_ref[...] = held[0:rows, :].astype(bf16)
    b_ref[0:rest, :] = held[rows:, :].astype(bf16)
    b_ref[rest:, :] = jnp.zeros((b_ref.shape[0] - rest, b_ref.shape[1]), bf16)
    whole_ref[0:rows, :] = a_ref[...]
    whole_ref[rows:, :] = b_ref[...]


def norm_kernel(count_ref, hidden_ref, normed_ref, mean_ref, inv_ref, fix_ref):
    tcount = jnp.full((1, fix_ref.shape[1]), count_ref[0].astype(f32))
    fix_ref[0:1, :] = 1.0 / (1.0 - jnp.exp(tcount * math.log(beta_one)))
    fix_ref[1:2, :] = 1.0 / (1.0 - jnp.exp(tcount * math.log(beta_two)))
    rows, width = hidden_ref.shape
    depth = normed_ref.shape[2]
    place = lax.axis_index("fsdp")
    step = 128
    for top in range(0, rows, step):
        part = pl.ds(top, step)
        values = hidden_ref[part, :].astype(f32)
        mean = jnp.mean(values, axis=-1, keepdims=True)
        center = values - mean
        inv = lax.rsqrt(jnp.mean(center * center, axis=-1, keepdims=True) + norm_eps)
        mean_ref[part, :] = mean
        inv_ref[part, :] = inv
        for slot in range(normed_ref.shape[0]):
            block = place ^ slot
            own = hidden_ref[part, columns(block, depth)].astype(f32)
            normed_ref[slot, part, :] = ((own - mean) * inv).astype(bf16)


def tiled_kernel(params_ref, moment_ref, second_ref, params_out, moment_out, second_out, sems):
    copies = []
    for slot, (src, dst) in enumerate(
        ((params_ref, params_out), (moment_ref, moment_out), (second_ref, second_out))
    ):
        copies.append(pltpu.make_async_copy(src.at[:, 0, :], dst, sems.at[slot]))
        copies[-1].start()
    for copy in copies:
        copy.wait()


def capped_exp(raw):
    capped = jnp.tanh(raw * (1.0 / logit_cap))
    return capped, jnp.exp(logit_cap * capped)


def logits_kernel(own_ref, near_ref, far_a, cross_a, far_b, normed_ref, capped_a_ref, exp_a_ref, acc_b_ref):
    rows = far_a.shape[0]
    raw = nt_dot(own_ref[0:rows, :], normed_ref[0]) + nt_dot(near_ref[0:rows, :], normed_ref[1])
    raw = raw + nt_dot(far_a[...], normed_ref[2]) + nt_dot(cross_a[...], normed_ref[3])
    capped_a_ref[...], exp_a_ref[...] = capped_exp(raw)
    acc = nt_dot(own_ref[rows:, :], normed_ref[0]) + nt_dot(near_ref[rows:, :], normed_ref[1])
    acc_b_ref[...] = acc + nt_dot(far_b[...], normed_ref[2])


def head_kernel(vocab, capped_a_ref, exp_a_ref, acc_b_ref, cross_b, normed_ref, labels_ref,
                lg_a_ref, lg_b_ref, cross_a_ref, cross_b_ref):
    rows = capped_a_ref.shape[0]
    capped_b, exp_b = capped_exp(acc_b_ref[...] + nt_dot(cross_b[...], normed_ref[3]))
    ids = lax.broadcasted_iota(jnp.int32, exp_b.shape, 0) + rows
    exp_b = jnp.where(ids < vocab, exp_b, 0.0)
    exp_a = exp_a_ref[...]
    total = jnp.sum(exp_a, axis=0, keepdims=True) + jnp.sum(exp_b, axis=0, keepdims=True)
    scale = 1.0 / total
    for top, capped, part, lg_ref, out_ref in (
        (0, capped_a_ref[...], exp_a, lg_a_ref, cross_a_ref),
        (rows, capped_b, exp_b, lg_b_ref, cross_b_ref),
    ):
        ids = lax.broadcasted_iota(jnp.int32, part.shape, 0) + top
        onehot = (ids == labels_ref[...]).astype(f32)
        logit_grad = ((part * scale - onehot) * (1.0 - capped * capped)).astype(bf16)
        lg_ref[...] = logit_grad
        out_ref[...] = nn_dot(logit_grad, normed_ref[3]).astype(bf16)


def grads_kernel(lg_a, lg_b, normed_ref, own_a, own_b, near_a, near_b, far_a, far_b):
    for slot, outs in ((2, (far_a, far_b)), (1, (near_a, near_b)), (0, (own_a, own_b))):
        for lg, out in zip((lg_a, lg_b), outs):
            out[...] = nn_dot(lg[...], normed_ref[slot]).astype(bf16)


def add_kernel(a_ref, b_ref, out_ref):
    out_ref[...] = (a_ref[...].astype(f32) + b_ref[...].astype(f32)).astype(bf16)


def hidden_grad_kernel(lg_a, lg_b, *refs):
    whole, weights_a, weights_b = refs[0:2], refs[2:4], refs[4:6]
    hidden_ref, mean_ref, inv_ref, out_ref, held = refs[6:]
    top = lg_a.shape[0]
    rows, width = hidden_ref.shape
    slots, _, depth = held.shape
    place = lax.axis_index("fsdp")
    mean, inv = mean_ref[...], inv_ref[...]
    first = jnp.zeros((rows, 1), f32)
    second = jnp.zeros((rows, 1), f32)
    for slot in range(slots):
        if slot < 2:
            block_a, block_b = whole[slot][0:top, :], whole[slot][top:, :]
        else:
            block_a, block_b = weights_a[slot - 2][...], weights_b[slot - 2][...]
        back = tn_dot(lg_a[...], block_a) + tn_dot(lg_b[...], block_b)
        held[slot] = back
        normalized = (hidden_ref[:, columns(place ^ slot, depth)].astype(f32) - mean) * inv
        first = first + jnp.sum(back, axis=-1, keepdims=True)
        second = second + jnp.sum(back * normalized, axis=-1, keepdims=True)
    first, second = first / width, second / width
    for slot in range(slots):
        part = columns(place ^ slot, depth)
        normalized = (hidden_ref[:, part].astype(f32) - mean) * inv
        out_ref[:, part] = (inv * (held[slot] - first - normalized * second)).astype(bf16)


def partial_sum_kernel(own_ref, near_ref, out_ref):
    out_ref[...] = own_ref[...].astype(f32) + near_ref[...].astype(f32)


def step_kernel(top, fix_ref, params_ref, moment_ref, second_ref, *refs):
    *terms, updated_ref, sent_ref, moment_out, second_out = refs
    rows = updated_ref.shape[0]
    part = pl.ds(top, rows)
    target = pl.ds(0, rows)
    grads = sum(ref[target, :].astype(f32) for ref in terms)
    moment_new = beta_one * moment_ref[part, :] + (1.0 - beta_one) * grads
    second_new = beta_two * second_ref[part, :] + (1.0 - beta_two) * grads * grads
    moment_out[...] = moment_new
    second_out[...] = second_new
    fix_one, fix_two = fix_ref[0:1, :], fix_ref[1:2, :]
    adam_step = moment_new * fix_one / (jnp.sqrt(second_new * fix_two) + adam_eps)
    params = params_ref[part, :]
    updated = params - learn_rate * (adam_step + weight_decay * params)
    updated_ref[...] = updated
    sent_ref[target, :] = updated.astype(bf16)
    rest = sent_ref.shape[0] - rows
    if rest:
        sent_ref[rows:, :] = jnp.zeros((rest, sent_ref.shape[1]), bf16)


def send_out(top, pairs, sems):
    copies = [
        pltpu.make_async_copy(source, target.at[pl.ds(top, source.shape[0]), 0, :], sems.at[slot])
        for slot, (source, target) in enumerate(pairs)
    ]
    for copy in copies:
        copy.start()
    return copies


def step_store_kernel(top, *refs):
    *ins, updated_ref, sent_ref, moment_out, second_out, held_moment, held_second, sems = refs
    step_kernel(top, *ins, updated_ref, sent_ref, held_moment, held_second)
    for copy in send_out(top, ((held_moment, moment_out), (held_second, second_out)), sems):
        copy.wait()


def store_kernel(top, moment_ref, second_ref, *refs):
    moment_out, second_out, sems = refs[-3:]
    for copy in send_out(top, ((moment_ref, moment_out), (second_ref, second_out)), sems):
        copy.wait()


def average_kernel(top, updated_ref, partner_ref, *refs):
    out_ref, held, sems = refs[-3:]
    rows = held.shape[0]
    held[...] = 0.5 * (updated_ref[...] + partner_ref[0:rows, :].astype(f32))
    for copy in send_out(top, ((held, out_ref),), sems):
        copy.wait()


def between_kernel(top, moment_ref, second_ref, updated_ref, partner_ref, *refs):
    moment_out, second_out, out_ref, held, sems = refs[-5:]
    copies = send_out(top, ((moment_ref, moment_out), (second_ref, second_out)), sems)
    held[...] = 0.5 * (updated_ref[...] + partner_ref[0 : held.shape[0], :].astype(f32))
    copies.append(pltpu.make_async_copy(held, out_ref.at[pl.ds(0, held.shape[0]), 0, :], sems.at[2]))
    copies[-1].start()
    for copy in copies:
        copy.wait()


def by_vocab(shard):
    return jnp.transpose(shard, (2, 0, 1))


def line_step(bit, hidden, targets, params, moment, second, train_step):
    tokens, width = hidden.shape[1:]
    depth, vocab = params.shape[1:]
    padded = -(-vocab // 16) * 16
    state_t = [by_vocab(shard) for shard in (params, moment, second)]
    heights = (chunk_rows, padded - chunk_rows)
    tops = (0, chunk_rows)
    counts = (chunk_rows, vocab - chunk_rows)
    shards = [shaped((height, depth), bf16) for height in heights]
    held = [pltpu.VMEM((count, depth), f32) for count in counts]
    state = shaped((vocab, depth), f32)
    state_out = pltpu.HBM((vocab, 1, depth), f32)
    dot_flops = 2 * padded * tokens * depth

    def hop(block, route):
        return lax.ppermute(block, "fsdp", route)

    whole_shard = shaped((padded, depth), bf16)
    *own, own_whole = run(
        round_weight_kernel,
        [hbm],
        [*shards, whole_shard],
        (state_t[0],),
        [pltpu.VMEM((vocab, depth), f32), dma((4,))],
    )
    far = [hop(block, far_route) for block in own]
    near = hop(own_whole, near_route)
    normed, mean, inv, fix = run(
        norm_kernel,
        [smem, vmem],
        [shaped((4, tokens, depth), bf16), shaped((tokens, 1), f32), shaped((tokens, 1), f32), shaped((2, depth), f32)],
        (train_step, hidden[0]),
        flops=10 * tokens * width,
        moved=4 * tokens * width,
    )
    tiled = run(tiled_kernel, [hbm] * 3, [state] * 3, state_t, [dma((3,))])
    far[0], normed, *tiled = lax.optimization_barrier((far[0], normed, *tiled))
    cross = [hop(block, near_route) for block in far]
    capped_a, exp_a, acc_b = run(
        logits_kernel,
        [vmem] * 6,
        [shaped((height, tokens), f32) for height in (heights[0], *heights)],
        (own_whole, near, far[0], cross[0], far[1], normed),
        flops=3 * dot_flops,
    )
    lg_a, lg_b, cross_part_a, cross_part_b = run(
        lambda *refs: head_kernel(vocab, *refs),
        [vmem] * 6,
        [shaped((height, tokens), bf16) for height in heights] + shards,
        (capped_a, exp_a, acc_b, cross[1], normed, targets),
        flops=2 * dot_flops,
    )
    got_a, got_b = [hop(block, near_route) for block in (cross_part_a, cross_part_b)]
    own_a, own_b, near_a, near_b, far_a, far_b = run(
        grads_kernel, [vmem] * 3, shards * 3, (lg_a, lg_b, normed), flops=3 * dot_flops
    )
    sum_a = run(add_kernel, [vmem] * 2, [shards[0]], (far_a, got_a))[0]
    near_a, later_a = lax.optimization_barrier((near_a, sum_a))
    got_far_a, got_near_a = hop(sum_a, far_route), hop(near_a, near_route)
    got_b, later_a = lax.optimization_barrier((got_b, later_a))
    sum_b = run(add_kernel, [vmem] * 2, [shards[1]], (far_b, got_b))[0]
    lg_late, sum_b = lax.optimization_barrier((lg_a, sum_b))
    grad_hidden = run(
        hidden_grad_kernel,
        [vmem] * 11,
        [shaped((tokens, width), bf16)],
        (lg_late, lg_b, own_whole, near, far[0], cross[0], far[1], cross[1], hidden[0], mean, inv),
        [pltpu.VMEM((4, tokens, depth), f32)],
        flops=4 * dot_flops,
    )[0]
    state_part = [shaped((count, depth), f32) for count in counts]
    if bit:
        sums = [shaped(shard.shape, f32) for shard in shards]
        local_a = run(partial_sum_kernel, [vmem] * 2, sums[:1], (own_a, got_near_a))[0]
        got_far_a, local_a, sum_b, near_b, grad_hidden = lax.optimization_barrier(
            (got_far_a, local_a, sum_b, near_b, grad_hidden)
        )
        got_near_b, got_far_b = hop(near_b, near_route), hop(sum_b, far_route)
        local_b = run(partial_sum_kernel, [vmem] * 2, sums[1:], (own_b, got_near_b))[0]
        terms = ((local_a, got_far_a), (local_b, got_far_b))
    else:
        got_far_a, grad_hidden = lax.optimization_barrier((got_far_a, grad_hidden))
        got_near_b, got_far_b = hop(near_b, near_route), hop(sum_b, far_route)
        sums = [shaped(shard.shape, f32) for shard in shards]
        local_a = run(partial_sum_kernel, [vmem] * 2, sums[:1], (own_a, got_near_a))[0]
        local_b = run(partial_sum_kernel, [vmem] * 2, sums[1:], (own_b, got_near_b))[0]
        terms = ((local_a, got_far_a), (local_b, got_far_b))
    moments, averaged = [], []

    def step(index, kernel, state_new, scratch=()):
        updated, sent, *state_new = run(
            functools.partial(kernel, tops[index]),
            [vmem] * (4 + len(terms[index])),
            [state_part[index], shards[index], *state_new],
            (fix, *tiled, *terms[index]),
            scratch,
            out_specs=[vmem, vmem] + [hbm if scratch else vmem] * 2,
        )
        return updated, from_partner(sent, "replica", bit), state_new

    def store(index, state_new, moments):
        return run(
            functools.partial(store_kernel, tops[index]),
            [vmem] * 2 + [hbm] * len(moments),
            [state_out] * 2,
            (*state_new, *moments),
            [dma((2,))],
            out_specs=[hbm] * 2,
            alias={2: 0, 3: 1} if moments else None,
        )

    def average(index, updated, partner, averaged):
        return run(
            functools.partial(average_kernel, tops[index]),
            [vmem] * 2 + [hbm] * len(averaged),
            [state_out],
            (updated, partner, *averaged),
            [held[index], dma((1,))],
            out_specs=[hbm],
            alias={2: 0} if averaged else None,
        )

    if bit:
        updated_a, partner_a, state_a = step(0, step_kernel, state_part[:1] * 2)
    else:
        scratch = [held[0], held[0], dma((2,))]
        updated_a, partner_a, moments = step(0, step_store_kernel, [state_out] * 2, scratch)
    updated_b, partner_b, state_b = step(1, step_kernel, state_part[1:] * 2)
    partner_a, updated_b = lax.optimization_barrier((partner_a, updated_b))
    if bit:
        averaged = average(0, updated_a, partner_a, averaged)
        moments = store(0, state_a, moments)
        moments = store(1, state_b, moments)
    else:
        *moments, averaged = run(
            functools.partial(between_kernel, tops[1]),
            [vmem] * 4 + [hbm] * 2,
            [state_out] * 3,
            (*state_b, updated_a, partner_a, *moments),
            [held[0], dma((3,))],
            out_specs=[hbm] * 3,
            alias={4: 0, 5: 1},
        )
        averaged = [averaged]
    averaged = average(1, updated_b, partner_b, averaged)
    outs = [jnp.transpose(out, (1, 2, 0)) for out in (averaged[0], *moments)]
    return (*outs, grad_hidden[None])


def local_line(hidden, targets, params, moment, second, train_step):
    levels = lax.axis_size("replica").bit_length() - 1
    branches = [functools.partial(line_step, bit) for bit in range(levels)]
    level = lax.rem(train_step[0], levels)
    return lax.switch(level, branches, hidden, targets, params, moment, second, train_step)


def local(hidden, targets, params, moment, second, train_step):
    four = lax.axis_size("fsdp") == 4 and params.shape[1] % 128 == 0 and hidden.shape[1] % 128 == 0
    four = four and params.shape[2] > chunk_rows
    chosen = local_line if four else local_any
    return chosen(hidden, targets, params, moment, second, train_step)


def solution(mesh):
    placed = (
        P("replica", ("groups", "fsdp"), None),
        P("replica", ("groups", "fsdp")),
        P("replica", ("groups", "fsdp"), None),
        P("replica", ("groups", "fsdp"), None),
        P("replica", ("groups", "fsdp"), None),
        P(),
    )
    return jax.shard_map(
        local,
        mesh=mesh,
        in_specs=placed,
        out_specs=(
            P("replica", ("groups", "fsdp"), None),
            P("replica", ("groups", "fsdp"), None),
            P("replica", ("groups", "fsdp"), None),
            P("replica", ("groups", "fsdp"), None),
        ),
        check_vma=False,
    )
```
